32 devices in a mesh: ctx: 4 (over y, x), mem: 8 (over z, core).
Axes of the slice: x: 2, y: 2, z: 4, core: 2. Of those that a mesh axis runs over, the one named last changes fastest.
Arguments:
- queries: bfloat16 [1536, 4096], P('ctx', 'mem'), may hold values from -6 to 6
- keys: bfloat16 [1536, 4096], P('ctx', 'mem'), may hold values from -6 to 6
- values: bfloat16 [1536, 4096], P('ctx', 'mem'), may hold values from -6 to 6
- out_grad: bfloat16 [1536, 4096], P('ctx', 'mem'), may hold values from -6 to 6
- mem_keys: bfloat16 [1024, 4096], P('mem'), may hold values from -6 to 6
- mem_values: bfloat16 [1024, 4096], P('mem'), may hold values from -6 to 6
- gate_logit: float32 [32], P('mem'), may hold values from -3 to 3
- block_ids: int32 [12, 4], P('ctx'), may hold values from 0 to 7, all different within a row
Outputs:
- mixed: bfloat16 [1536, 4096], P('ctx', 'mem')
- query_grad: bfloat16 [1536, 4096], P('ctx', 'mem')
- mem_key_grad: bfloat16 [1024, 4096], P('mem', 'ctx')
- mem_value_grad: bfloat16 [1024, 4096], P('mem', 'ctx')
The draws below stay inside these ranges and needn't reach their ends.
Inputs may be any that keep to these rules, and one draw needn't show every extreme that they name: `block_ids`: the 4 ids listed for one query block are distinct, and every memory block is listed somewhere.
All inputs are finite; a program needn't handle non-finite values.
Results may differ from the reference program's by a relative error of at most 0.02.
Values may be sent and summed in bfloat16 or wider, within the bound.
A program may use at most 64 MiB of HBM per device.

```python
import jax
import jax.numpy as jnp
from jax import lax

HEADS = 32
HEAD_SIZE = 128
D = 4096
BLOCK = 128
LIST = 4
TOK_DEV = 384
SEQUENCE_TOKENS = 1536
NQB = 12
MEM_BLOCKS = 8
MEM_ROWS = 1024
N_CTX = 4


def draw_queries(key, part):
    drawn = jnp.clip(jax.random.normal(jax.random.fold_in(key, 11), (SEQUENCE_TOKENS, D), jnp.float32), -6.0, 6.0)
    return drawn.astype(jnp.bfloat16)


def draw_keys(key, part):
    drawn = jnp.clip(jax.random.normal(jax.random.fold_in(key, 12), (SEQUENCE_TOKENS, D), jnp.float32), -6.0, 6.0)
    return drawn.astype(jnp.bfloat16)


def draw_mem_keys(key, part):
    drawn = jnp.clip(jax.random.normal(jax.random.fold_in(key, 13), (MEM_ROWS, D), jnp.float32), -6.0, 6.0)
    return drawn.astype(jnp.bfloat16)


def levels(rng, extent, cuts, low, top_value):
    factor_of = 1.0
    for position, blocks in cuts:
        draws = jax.random.uniform(jax.random.fold_in(jax.random.fold_in(rng, 6), position), (blocks,), jnp.float32, low / len(cuts), top_value / len(cuts))
        factor_of = factor_of * jnp.repeat(jnp.exp(draws), extent[position] // blocks).reshape((-1,) + (1,) * (len(extent) - 1 - position))
    return factor_of


def different_ones(own_key, rows, count, top, lift):
    order = jax.random.permutation(jax.random.fold_in(own_key, 1), count)
    favour = order
    for power in range(3):
        favour = favour * favour // count
    favour = favour * lift // count
    chance = jax.random.randint(jax.random.fold_in(own_key, 2), (rows, count), 0, 4096) + favour
    sure = jax.random.permutation(jax.random.fold_in(own_key, 3), rows)[jnp.arange(count) % rows]
    chance = jnp.where(jnp.arange(rows)[:, None] == sure[None, :], 1 << 14, chance)
    score = chance * count + jnp.arange(count)
    return lax.top_k(score.astype(jnp.int32), top)[1].astype(jnp.int32)


def centred(key, shape, spread, most, cuts=(), kind=jnp.bfloat16):
    values = jax.random.normal(key, shape, jnp.float32) * spread
    if len(cuts) > 0:
        values = levels(key, shape, cuts, -0.22, 0.18) * values
    return jnp.clip(values, min=-most, max=most).astype(kind)


def setup_inputs(seed: int = 0) -> dict:
    streams_of = jax.random.split(jax.random.key(seed), 9)
    return {
        "queries": draw_queries(jax.random.fold_in(streams_of[8], 71), 0),
        "keys": draw_keys(jax.random.fold_in(streams_of[8], 71), 0),
        "values": centred(streams_of[2], (SEQUENCE_TOKENS, D), 1.0, 6.0, ((0, 4), (1, 8))),
        "out_grad": centred(streams_of[3], (SEQUENCE_TOKENS, D), 1.0, 6.0, ((0, 4), (1, 8))),
        "mem_keys": draw_mem_keys(jax.random.fold_in(streams_of[8], 71), 0),
        "mem_values": centred(streams_of[5], (MEM_ROWS, D), 1.0, 6.0, ((0, 8),)),
        "gate_logit": jnp.clip(jax.random.uniform(streams_of[6], (HEADS,), jnp.float32, -3.0, 3.0) * levels(streams_of[6], (HEADS,), ((0, 8),), -0.4, 0.0), -3.0, 3.0),
        "block_ids": different_ones(streams_of[7], NQB, MEM_BLOCKS, LIST, 8192),
    }


def rounded(array):
    return lax.optimization_barrier(array.astype(jnp.bfloat16)).astype(jnp.float32)


def head_pass(inputs, block_ids):
    query, key_rows, value_rows, grad_rows, memory_keys, memory_values, gate_share = inputs
    scores_scale_factor = HEAD_SIZE ** -0.5
    positions = jnp.arange(SEQUENCE_TOKENS)
    causal = positions[None, :] <= positions[:, None]
    scores = jnp.dot(query, key_rows.T, preferred_element_type=jnp.float32) * scores_scale_factor
    masked = jnp.where(causal, scores, -1e30)
    row_max = jnp.max(masked, axis=-1)
    exp_terms = jnp.where(causal, jnp.exp(masked - row_max[:, None]), 0.0)
    row_total = jnp.sum(exp_terms, axis=-1)
    local_out = jnp.dot(exp_terms.astype(jnp.bfloat16), value_rows, preferred_element_type=jnp.float32) / row_total[:, None]
    log_total = row_max + jnp.log(row_total)

    query_block_list = query.reshape(NQB, BLOCK, HEAD_SIZE).astype(jnp.float32)
    selected_keys = memory_keys.reshape(MEM_BLOCKS, BLOCK, HEAD_SIZE)[block_ids].reshape(NQB, LIST * BLOCK, HEAD_SIZE).astype(jnp.float32)
    selected_values = memory_values.reshape(MEM_BLOCKS, BLOCK, HEAD_SIZE)[block_ids].reshape(NQB, LIST * BLOCK, HEAD_SIZE).astype(jnp.float32)
    memory_score_matrix = jnp.einsum("iom,ipm->iop", query_block_list, selected_keys) * scores_scale_factor
    weights = jax.nn.softmax(memory_score_matrix, axis=-1)
    weights_reduced = rounded(weights)
    memory_output = jnp.einsum("plz,pzr->plr", weights_reduced, selected_values).reshape(SEQUENCE_TOKENS, HEAD_SIZE)
    mixed = (gate_share * memory_output + (1.0 - gate_share) * local_out).astype(jnp.bfloat16)

    grad_full = grad_rows.astype(jnp.float32)
    grad_mem = gate_share * grad_full
    grad_local = (1.0 - gate_share) * grad_full
    probs = jnp.where(causal, jnp.exp(masked - log_total[:, None]), 0.0)
    grad_probs = jnp.dot(grad_local.astype(jnp.bfloat16), value_rows.T, preferred_element_type=jnp.float32)
    local_delta = jnp.sum(grad_local * local_out, axis=-1)
    grad_scores = probs * (grad_probs - local_delta[:, None])
    local_grad = jnp.dot(grad_scores.astype(jnp.bfloat16), key_rows, preferred_element_type=jnp.float32) * scores_scale_factor

    memory_gradient_reduced = rounded(grad_mem).reshape(NQB, BLOCK, HEAD_SIZE)
    weight_gradient = jnp.einsum("iom,ipm->iop", memory_gradient_reduced, selected_values)
    mem_delta = jnp.sum(grad_mem * memory_output, axis=-1).reshape(NQB, BLOCK)
    memory_score_gradient = rounded(weights * (weight_gradient - mem_delta[:, :, None]))
    memory_gradient = jnp.einsum("plz,pzr->plr", memory_score_gradient, selected_keys).reshape(SEQUENCE_TOKENS, HEAD_SIZE) * scores_scale_factor
    selected_key_gradient = jnp.einsum("spn,spu->snu", memory_score_gradient, query_block_list) * scores_scale_factor
    selected_value_gradient = jnp.einsum("spn,spu->snu", weights_reduced, memory_gradient_reduced)
    query_grad = (memory_gradient + local_grad).astype(jnp.bfloat16)

    per_segment = TOK_DEV // BLOCK * LIST
    seg_keys = selected_key_gradient.reshape(N_CTX, per_segment, BLOCK, HEAD_SIZE)
    seg_values = selected_value_gradient.reshape(N_CTX, per_segment, BLOCK, HEAD_SIZE)
    seg_ids = block_ids.reshape(N_CTX, per_segment)
    block_numbers = jnp.arange(MEM_BLOCKS).astype(jnp.int32)

    def add_segment(totals, pieces):
        piece_keys, piece_values, piece_ids = pieces
        one_hot = (piece_ids[:, None] == block_numbers[None, :]).astype(jnp.float32)
        part_keys = jnp.einsum("jb,jrd->brd", one_hot, piece_keys, precision=lax.Precision.HIGHEST)
        part_values = jnp.einsum("jb,jrd->brd", one_hot, piece_values, precision=lax.Precision.HIGHEST)
        return (totals[0] + rounded(part_keys), totals[1] + rounded(part_values)), None

    empty = jnp.zeros((MEM_BLOCKS, BLOCK, HEAD_SIZE), jnp.float32)
    (key_total, value_total), _ = lax.scan(add_segment, (empty, empty), (seg_keys, seg_values, seg_ids))
    return (mixed, query_grad, key_total.reshape(MEM_ROWS, HEAD_SIZE).astype(jnp.bfloat16),
            value_total.reshape(MEM_ROWS, HEAD_SIZE).astype(jnp.bfloat16))


def heads_first(array, row_count):
    return array.reshape(row_count, HEADS, HEAD_SIZE).transpose(1, 0, 2)


def rows_first(array, row_count):
    return array.transpose(1, 0, 2).reshape(row_count, D)


def reference(queries, keys, values, out_grad, mem_keys, mem_values, gate_logit, block_ids):
    gate_values = jax.nn.sigmoid(gate_logit.astype(jnp.float32))
    stacked = (heads_first(queries, SEQUENCE_TOKENS), heads_first(keys, SEQUENCE_TOKENS), heads_first(values, SEQUENCE_TOKENS),
               heads_first(out_grad, SEQUENCE_TOKENS), heads_first(mem_keys, MEM_ROWS), heads_first(mem_values, MEM_ROWS),
               gate_values)
    mixed, query_grad, key_grad, value_grad = lax.map(lambda inputs: head_pass(inputs, block_ids), stacked)
    return (rows_first(mixed, SEQUENCE_TOKENS), rows_first(query_grad, SEQUENCE_TOKENS),
            rows_first(key_grad, MEM_ROWS), rows_first(value_grad, MEM_ROWS))
```

```python
import functools
import math

import jax
import jax.numpy as jnp
from jax import lax
from jax.experimental import pallas as pl
from jax.experimental.pallas import tpu as pltpu
from jax.sharding import PartitionSpec as P

HEAD_SIZE = 128
BLOCK = 128
MESH = pl.DeviceIdType.MESH
NEG = -1e30
F32 = jnp.float32
BF16 = jnp.bfloat16


def dot_nt(a, b):
    return lax.dot_general(a, b, (((1,), (1,)), ((), ())), preferred_element_type=F32)


def dot_nn(a, b):
    return lax.dot_general(a, b, (((1,), (0,)), ((), ())), preferred_element_type=F32)


def dot_tn(a, b):
    return lax.dot_general(a, b, (((0,), (0,)), ((), ())), preferred_element_type=F32)


def loop(low, high, body):
    def step(i, carry):
        body(i)
        return carry

    lax.fori_loop(low, high, step, 0)


def kernel(n_ctx, n_mem, ids, gate, q_ref, k_ref, v_ref, do_ref, mk_ref, mv_ref,
           mixed_ref, qg_ref, gk_ref, gv_ref,
           kall, vall, fk, fv, parts, recv, red, out, s_loc, s_mem,
           own_sem, fsend, frecv, lsend, lrecv, psend, precv, osend, orecv):
    c = lax.axis_index("ctx")
    m = lax.axis_index("mem")
    tok, width = q_ref.shape
    heads = width // HEAD_SIZE
    nqb = tok // BLOCK
    n_list = ids.shape[1]
    per = n_mem // n_ctx
    nsub = n_ctx // 2
    rs = BLOCK // nsub
    group = m // per
    col0 = lax.rem(m, per) * width
    scale = HEAD_SIZE ** -0.5
    scale2 = scale * math.log2(math.e)
    chunk = 2 * BLOCK
    n_chunk = n_mem * BLOCK // chunk

    def head(h, base=0):
        return pl.ds(pl.multiple_of(base + h * HEAD_SIZE, HEAD_SIZE), HEAD_SIZE)

    def rows(start, size):
        return pl.ds(pl.multiple_of(start, size), size)

    barrier = pltpu.get_barrier_semaphore()

    def greet(ctx, mem):
        pl.semaphore_signal(barrier, inc=1, device_id={"ctx": ctx, "mem": mem}, device_id_type=MESH)

    loop(1, n_mem, lambda d: greet(c, lax.rem(m + d, n_mem)))
    loop(1, n_ctx, lambda d: greet(lax.rem(c + d, n_ctx), m))

    def greet_owner(t):
        src_c, src_m = t // per, c * per + lax.rem(t, per)

        @pl.when(jnp.logical_or(src_c != c, src_m != m))
        def _():
            greet(src_c, src_m)

    loop(0, n_ctx * per, greet_owner)
    own_k = pltpu.make_async_copy(mk_ref.at[:, rows(m * width, width)], fk.at[rows(m * BLOCK, BLOCK)], own_sem.at[0])
    own_v = pltpu.make_async_copy(mv_ref.at[:, rows(m * width, width)], fv.at[rows(m * BLOCK, BLOCK)], own_sem.at[1])
    own_k.start()
    own_v.start()
    kall[c] = k_ref[...]
    vall[c] = v_ref[...]
    pl.semaphore_wait(barrier, n_mem - 1 + n_ctx - 1 + n_mem - jnp.where(group == c, 1, 0))

    def fetch(which, h, p):
        src, dst = ((mk_ref, fk), (mv_ref, fv))[which]
        return pltpu.make_async_remote_copy(
            src_ref=src.at[:, head(h, p * width)], dst_ref=dst.at[rows(m * BLOCK, BLOCK), head(h)],
            send_sem=fsend.at[which, h, p], recv_sem=frecv.at[which, h, m],
            device_id={"ctx": c, "mem": p}, device_id_type=MESH)

    def fetched(which, h, p):
        src, dst = ((mk_ref, fk), (mv_ref, fv))[which]
        return pltpu.make_async_remote_copy(
            src_ref=src.at[:, head(h, p * width)], dst_ref=dst.at[rows(p * BLOCK, BLOCK), head(h)],
            send_sem=fsend.at[which, h, p], recv_sem=frecv.at[which, h, p],
            device_id={"ctx": c, "mem": p}, device_id_type=MESH)

    def share(which, h, p, slot):
        src, dst = ((k_ref, kall), (v_ref, vall))[which]
        return pltpu.make_async_remote_copy(
            src_ref=src.at[:, head(h)], dst_ref=dst.at[slot, :, head(h)],
            send_sem=lsend.at[which, h, p], recv_sem=lrecv.at[which, h, slot],
            device_id={"ctx": p, "mem": m}, device_id_type=MESH)

    def part(h, p, slot):
        return pltpu.make_async_remote_copy(
            src_ref=parts.at[p, :, :, head(h)], dst_ref=recv.at[slot, :, :, head(h)],
            send_sem=psend.at[h, p], recv_sem=precv.at[h, slot],
            device_id={"ctx": p, "mem": m}, device_id_type=MESH)

    def owner_copy(h, r, src_c, src_i, base):
        return pltpu.make_async_remote_copy(
            src_ref=red.at[r, :, head(h)],
            dst_ref=out.at[src_c // nsub, rows(lax.rem(src_c, nsub) * rs, rs), head(h, base)],
            send_sem=osend.at[h, r], recv_sem=orecv.at[h, src_c, src_i],
            device_id={"ctx": group, "mem": r}, device_id_type=MESH)

    def start_head(h):
        def to_mem(d):
            p = lax.rem(m + d, n_mem)
            fetch(0, h, p).start()
            fetch(1, h, p).start()

        def to_ctx(p):
            share(0, h, p, c).start()
            share(1, h, p, c).start()

        loop(c + 1, n_ctx, to_ctx)
        loop(1, n_mem, to_mem)

    loop(0, heads, start_head)
    own_k.wait()
    own_v.wait()

    difference = (lax.broadcasted_iota(jnp.int32, (tok, tok), 1)
                  - lax.broadcasted_iota(jnp.int32, (tok, tok), 0))

    def listed(b, r):
        hit = ids[b, 0] == r
        for j in range(1, n_list):
            hit = jnp.logical_or(hit, ids[b, j] == r)
        return jnp.where(hit, 0.0, NEG).astype(F32)

    def reduce_head(h):
        total = parts[c, :, :, head(h)].astype(F32)

        def add(d, total):
            src = lax.rem(c + d, n_ctx)
            part(h, src, src).wait_recv()
            return total + recv[src, :, :, head(h)].astype(F32)

        total = lax.fori_loop(1, n_ctx, add, total)
        red[:, :, head(h)] = total.astype(BF16)

        def send(d):
            r = lax.rem(m + d, n_mem)
            owner_copy(h, r, c, lax.rem(m, per), col0).start()

        loop(1, n_mem, send)

        @pl.when(group == c)
        def _():
            out[c // nsub, rows(lax.rem(c, nsub) * rs, rs), head(h, col0)] = red[m, :, head(h)]

        @pl.when(group != c)
        def _():
            owner_copy(h, m, c, lax.rem(m, per), col0).start()

    def one_head(h):
        hc = head(h)
        q = q_ref[:, hc]
        g = 1.0 / (1.0 + jnp.exp(-jnp.full((1, HEAD_SIZE), gate[h], F32)))
        grad = do_ref[:, hc].astype(F32)
        dl = (1.0 - g) * grad
        dl_low = dl.astype(BF16)

        def wait_local(j):
            share(0, h, j, j).wait_recv()
            share(1, h, j, j).wait_recv()

        loop(0, c, wait_local)

        def scores(j, top):
            s = dot_nt(q, kall[j, :, hc]) * scale2
            s = jnp.where(difference <= (c - j) * tok, s, NEG)
            s_loc[j] = s
            return jnp.maximum(top, jnp.max(s, axis=-1, keepdims=True))

        top = lax.fori_loop(0, c + 1, scores, jnp.full((tok, 1), NEG, F32))

        def gather(j, carry):
            total, acc = carry
            e = jnp.exp2(s_loc[j] - top)
            s_loc[j] = e
            return (total + jnp.sum(e, axis=-1, keepdims=True),
                    acc + dot_nn(e.astype(BF16), vall[j, :, hc]))

        total, acc = lax.fori_loop(0, c + 1, gather, (jnp.zeros((tok, 1), F32), jnp.zeros((tok, HEAD_SIZE), F32)))
        inv = 1.0 / total
        local_out = acc * inv
        delta = jnp.sum(dl * local_out, axis=-1, keepdims=True)

        def back(j, acc):
            dp = dot_nt(dl_low, vall[j, :, hc])
            ds = (s_loc[j] * inv) * (dp - delta)
            return acc + dot_nn(ds.astype(BF16), kall[j, :, hc])

        local_grad = lax.fori_loop(0, c + 1, back, jnp.zeros((tok, HEAD_SIZE), F32))

        def wait_memory(d):
            p = lax.rem(m + d, n_mem)
            fetched(0, h, p).wait_recv()
            fetched(1, h, p).wait_recv()

        loop(1, n_mem, wait_memory)
        dm = g * grad
        dm_low = dm.astype(BF16)

        def mem_scores(i, top):
            s = dot_nt(q, fk[rows(i * chunk, chunk), hc]) * scale2
            bias = jnp.concatenate(
                [jnp.concatenate([jnp.full((BLOCK, BLOCK), listed(b, 2 * i + x), F32) for x in range(2)], axis=1)
                 for b in range(nqb)], axis=0)
            s = s + bias
            s_mem[i] = s
            return jnp.maximum(top, jnp.max(s, axis=-1, keepdims=True))

        top2 = lax.fori_loop(0, n_chunk, mem_scores, jnp.full((tok, 1), NEG, F32))

        def mem_gather(i, carry):
            total, acc = carry
            e = jnp.exp2(s_mem[i] - top2)
            s_mem[i] = e
            return (total + jnp.sum(e, axis=-1, keepdims=True),
                    acc + dot_nn(e.astype(BF16), fv[rows(i * chunk, chunk), hc]))

        total2, acc2 = lax.fori_loop(0, n_chunk, mem_gather,
                                     (jnp.zeros((tok, 1), F32), jnp.zeros((tok, HEAD_SIZE), F32)))
        inv2 = 1.0 / total2
        mem_out = acc2 * inv2
        mixed_ref[:, hc] = (g * mem_out + (1.0 - g) * local_out).astype(BF16)
        delta2 = jnp.sum(dm * mem_out, axis=-1, keepdims=True)

        def mem_back(i, acc):
            dw = dot_nt(dm_low, fv[rows(i * chunk, chunk), hc])
            w = s_mem[i] * inv2
            ds = (w * (dw - delta2)).astype(BF16)
            part_k = (dot_tn(ds, q) * scale).astype(BF16)
            part_v = dot_tn(w.astype(BF16), dm_low).astype(BF16)
            for x in range(2):
                for s in range(nsub):
                    at = slice(x * BLOCK + s * rs, x * BLOCK + (s + 1) * rs)
                    parts[s, 2 * i + x, :, hc] = part_k[at]
                    parts[nsub + s, 2 * i + x, :, hc] = part_v[at]
            return acc + dot_nn(ds, fk[rows(i * chunk, chunk), hc])

        mem_grad = lax.fori_loop(0, n_chunk, mem_back, jnp.zeros((tok, HEAD_SIZE), F32))
        qg_ref[:, hc] = ((local_grad + mem_grad) * scale).astype(BF16)

        loop(1, n_ctx, lambda d: part(h, lax.rem(c + d, n_ctx), c).start())

        @pl.when(h > 0)
        def _():
            reduce_head(h - 1)

    loop(0, heads, one_head)
    reduce_head(heads - 1)

    def finish(h):
        def arrived(t):
            src_c, i = t // per, lax.rem(t, per)

            @pl.when(jnp.logical_or(src_c != c, c * per + i != m))
            def _():
                owner_copy(h, m, src_c, i, i * width).wait_recv()

        def sent_mem(d):
            p = lax.rem(m + d, n_mem)
            fetch(0, h, p).wait_send()
            fetch(1, h, p).wait_send()
            owner_copy(h, p, c, lax.rem(m, per), col0).wait_send()

        def sent_ctx(p):
            share(0, h, p, c).wait_send()
            share(1, h, p, c).wait_send()

        loop(0, n_ctx * per, arrived)
        loop(1, n_mem, sent_mem)
        loop(c + 1, n_ctx, sent_ctx)
        loop(1, n_ctx, lambda d: part(h, lax.rem(c + d, n_ctx), c).wait_send())

        @pl.when(group != c)
        def _():
            owner_copy(h, m, c, lax.rem(m, per), col0).wait_send()

    loop(0, heads, finish)
    gk_ref[...] = out[0]
    gv_ref[...] = out[1]


def shards(n_ctx, n_mem, queries, keys, values, out_grad, mem_keys, mem_values, gate_logit, block_ids):
    tok, width = queries.shape
    columns = mem_keys.shape[1]
    heads = width // HEAD_SIZE
    rs = 2 * BLOCK // n_ctx
    mem_rows = n_mem * BLOCK
    vmem = pl.BlockSpec(memory_space=pltpu.VMEM)
    smem = pl.BlockSpec(memory_space=pltpu.SMEM)
    hbm = pl.BlockSpec(memory_space=pl.ANY)
    dma = pltpu.SemaphoreType.DMA
    pairs = (n_ctx + 1) * tok * tok * heads * HEAD_SIZE
    return pl.pallas_call(
        functools.partial(kernel, n_ctx, n_mem),
        out_shape=(
            jax.ShapeDtypeStruct((tok, width), BF16),
            jax.ShapeDtypeStruct((tok, width), BF16),
            jax.ShapeDtypeStruct((BLOCK, columns // n_ctx), BF16),
            jax.ShapeDtypeStruct((BLOCK, columns // n_ctx), BF16),
        ),
        in_specs=[smem, smem, vmem, vmem, vmem, vmem, hbm, hbm],
        out_specs=(vmem, vmem, vmem, vmem),
        scratch_shapes=[
            pltpu.VMEM((n_ctx, tok, width), BF16),
            pltpu.VMEM((n_ctx, tok, width), BF16),
            pltpu.VMEM((mem_rows, width), BF16),
            pltpu.VMEM((mem_rows, width), BF16),
            pltpu.VMEM((n_ctx, n_mem, rs, width), BF16),
            pltpu.VMEM((n_ctx, n_mem, rs, width), BF16),
            pltpu.VMEM((n_mem, rs, width), BF16),
            pltpu.VMEM((2, BLOCK, columns // n_ctx), BF16),
            pltpu.VMEM((n_ctx, tok, tok), F32),
            pltpu.VMEM((mem_rows // (2 * BLOCK), tok, 2 * BLOCK), F32),
            dma((2,)),
            dma((2, heads, n_mem)), dma((2, heads, n_mem)),
            dma((2, heads, n_ctx)), dma((2, heads, n_ctx)),
            dma((heads, n_ctx)), dma((heads, n_ctx)),
            dma((heads, n_mem)), dma((heads, n_ctx, n_mem // n_ctx)),
        ],
        compiler_params=pltpu.CompilerParams(
            collective_id=0, has_side_effects=True, vmem_limit_bytes=48 * 1024 * 1024
        ),
        cost_estimate=pl.CostEstimate(
            flops=8 * pairs, bytes_accessed=8 * 1024 * 1024, transcendentals=4 * tok * tok * heads
        ),
    )(block_ids, gate_logit, queries, keys, values, out_grad, mem_keys, mem_values)


def solution(mesh):
    in_specs = (
        P("ctx", "mem"),
        P("ctx", "mem"),
        P("ctx", "mem"),
        P("ctx", "mem"),
        P("mem", None),
        P("mem", None),
        P("mem"),
        P("ctx", None),
    )
    out_specs = (P("ctx", "mem"), P("ctx", "mem"), P("mem", "ctx"), P("mem", "ctx"))
    body = functools.partial(shards, mesh.shape["ctx"], mesh.shape["mem"])
    return jax.shard_map(body, mesh=mesh, in_specs=in_specs, out_specs=out_specs, check_vma=False)
```

```python
import functools
import math

import jax
import jax.numpy as jnp
from jax import lax
from jax.experimental import pallas as pl
from jax.experimental.pallas import tpu as pltpu
from jax.sharding import PartitionSpec as P

HEAD_SIZE = 128
BLOCK = 128
MESH = pl.DeviceIdType.MESH
NEG = -1e30
F32 = jnp.float32
BF16 = jnp.bfloat16


def dot_nt(a, b):
    return lax.dot_general(a, b, (((1,), (1,)), ((), ())), preferred_element_type=F32)


def dot_nn(a, b):
    return lax.dot_general(a, b, (((1,), (0,)), ((), ())), preferred_element_type=F32)


def dot_tn(a, b):
    return lax.dot_general(a, b, (((0,), (0,)), ((), ())), preferred_element_type=F32)


def loop(low, high, body):
    def step(i, carry):
        body(i)
        return carry

    lax.fori_loop(low, high, step, 0)


def kernel(n_ctx, n_mem, ids_in, gate_in, q_in, k_ref, v_ref, do_in, mk_ref, mv_ref,
           mixed_ref, qg_ref, gk_ref, gv_ref,
           ids, gate, q_ref, do_ref, l_out, l_grad, m_out, m_grad, kall, vall, fk, fv, parts, recv, red, out, s_loc, s_mem,
           own_sem, fsend, frecv, lsend, lrecv, psend, precv, osend, orecv):
    c = lax.axis_index("ctx")
    m = lax.axis_index("mem")
    tok, width = q_in.shape
    heads = width // HEAD_SIZE
    nqb = tok // BLOCK
    n_list = ids.shape[1]
    per = n_mem // n_ctx
    nsub = n_ctx // 2
    rs = BLOCK // nsub
    group = m // per
    col0 = lax.rem(m, per) * width
    scale = HEAD_SIZE ** -0.5
    scale2 = scale * math.log2(math.e)
    chunk = 2 * BLOCK
    n_chunk = n_mem * BLOCK // chunk

    def head(h, base=0):
        return pl.ds(pl.multiple_of(base + h * HEAD_SIZE, HEAD_SIZE), HEAD_SIZE)

    def rows(start, size):
        return pl.ds(pl.multiple_of(start, size), size)

    barrier = pltpu.get_barrier_semaphore()

    def greet(ctx, mem):
        pl.semaphore_signal(barrier, inc=1, device_id={"ctx": ctx, "mem": mem}, device_id_type=MESH)

    loop(1, n_mem, lambda d: greet(c, lax.rem(m + d, n_mem)))
    loop(1, n_ctx, lambda d: greet(lax.rem(c + d, n_ctx), m))

    def greet_owner(t):
        src_c, src_m = t // per, c * per + lax.rem(t, per)

        @pl.when(jnp.logical_or(src_c != c, src_m != m))
        def _():
            greet(src_c, src_m)

    loop(0, n_ctx * per, greet_owner)
    own_k = pltpu.make_async_copy(mk_ref.at[:, rows(m * width, width)], fk.at[rows(m * BLOCK, BLOCK)], own_sem.at[0])
    own_v = pltpu.make_async_copy(mv_ref.at[:, rows(m * width, width)], fv.at[rows(m * BLOCK, BLOCK)], own_sem.at[1])
    mine = [
        pltpu.make_async_copy(ids_in, ids, own_sem.at[2]),
        pltpu.make_async_copy(gate_in, gate, own_sem.at[3]),
        pltpu.make_async_copy(q_in, q_ref, own_sem.at[4]),
        pltpu.make_async_copy(do_in, do_ref, own_sem.at[5]),
        pltpu.make_async_copy(k_ref, kall.at[c], own_sem.at[6]),
        pltpu.make_async_copy(v_ref, vall.at[c], own_sem.at[7]),
        own_k,
        own_v,
    ]
    for copy in mine:
        copy.start()
    pl.semaphore_wait(barrier, n_mem - 1 + n_ctx - 1 + n_mem - jnp.where(group == c, 1, 0))

    def fetch(which, h, p):
        src, dst = ((mk_ref, fk), (mv_ref, fv))[which]
        return pltpu.make_async_remote_copy(
            src_ref=src.at[:, head(h, p * width)], dst_ref=dst.at[rows(m * BLOCK, BLOCK), head(h)],
            send_sem=fsend.at[which, h, p], recv_sem=frecv.at[which, h, m],
            device_id={"ctx": c, "mem": p}, device_id_type=MESH)

    def fetched(which, h, p):
        src, dst = ((mk_ref, fk), (mv_ref, fv))[which]
        return pltpu.make_async_remote_copy(
            src_ref=src.at[:, head(h, p * width)], dst_ref=dst.at[rows(p * BLOCK, BLOCK), head(h)],
            send_sem=fsend.at[which, h, p], recv_sem=frecv.at[which, h, p],
            device_id={"ctx": c, "mem": p}, device_id_type=MESH)

    def share(which, h, p, slot):
        src, dst = ((k_ref, kall), (v_ref, vall))[which]
        return pltpu.make_async_remote_copy(
            src_ref=src.at[:, head(h)], dst_ref=dst.at[slot, :, head(h)],
            send_sem=lsend.at[which, h, p], recv_sem=lrecv.at[which, h, slot],
            device_id={"ctx": p, "mem": m}, device_id_type=MESH)

    def part(h, p, slot):
        return pltpu.make_async_remote_copy(
            src_ref=parts.at[p, :, :, head(h)], dst_ref=recv.at[slot, :, :, head(h)],
            send_sem=psend.at[h, p], recv_sem=precv.at[h, slot],
            device_id={"ctx": p, "mem": m}, device_id_type=MESH)

    def owner_copy(h, r, src_c, src_i, base):
        return pltpu.make_async_remote_copy(
            src_ref=red.at[r, :, head(h)],
            dst_ref=out.at[src_c // nsub, rows(lax.rem(src_c, nsub) * rs, rs), head(h, base)],
            send_sem=osend.at[h, r], recv_sem=orecv.at[h, src_c, src_i],
            device_id={"ctx": group, "mem": r}, device_id_type=MESH)

    def start_head(h):
        def to_mem(d):
            p = lax.rem(m + d, n_mem)
            fetch(0, h, p).start()
            fetch(1, h, p).start()

        def to_ctx(p):
            share(0, h, p, c).start()
            share(1, h, p, c).start()

        loop(c + 1, n_ctx, to_ctx)
        loop(1, n_mem, to_mem)

    loop(0, heads, start_head)
    for copy in mine:
        copy.wait()

    difference = (lax.broadcasted_iota(jnp.int32, (tok, tok), 1)
                  - lax.broadcasted_iota(jnp.int32, (tok, tok), 0))

    def listed(b, r):
        hit = ids[b, 0] == r
        for j in range(1, n_list):
            hit = jnp.logical_or(hit, ids[b, j] == r)
        return jnp.where(hit, 0.0, NEG).astype(F32)

    def reduce_head(h):
        total = parts[c, :, :, head(h)].astype(F32)

        def add(d, total):
            src = lax.rem(c + d, n_ctx)
            part(h, src, src).wait_recv()
            return total + recv[src, :, :, head(h)].astype(F32)

        total = lax.fori_loop(1, n_ctx, add, total)
        red[:, :, head(h)] = total.astype(BF16)

        def send(d):
            r = lax.rem(m + d, n_mem)
            owner_copy(h, r, c, lax.rem(m, per), col0).start()

        loop(1, n_mem, send)

        @pl.when(group == c)
        def _():
            out[c // nsub, rows(lax.rem(c, nsub) * rs, rs), head(h, col0)] = red[m, :, head(h)]

        @pl.when(group != c)
        def _():
            owner_copy(h, m, c, lax.rem(m, per), col0).start()

    def share_of_gate(h):
        return 1.0 / (1.0 + jnp.exp(-jnp.full((1, HEAD_SIZE), gate[h], F32)))

    def local_head(h):
        hc = head(h)
        q = q_ref[:, hc]
        g = share_of_gate(h)
        grad = do_ref[:, hc].astype(F32)
        dl = (1.0 - g) * grad
        dl_low = dl.astype(BF16)

        def wait_local(j):
            share(0, h, j, j).wait_recv()
            share(1, h, j, j).wait_recv()

        loop(0, c, wait_local)

        def scores(j, top):
            s = dot_nt(q, kall[j, :, hc]) * scale2
            s = jnp.where(difference <= (c - j) * tok, s, NEG)
            s_loc[j] = s
            return jnp.maximum(top, jnp.max(s, axis=-1, keepdims=True))

        top = lax.fori_loop(0, c + 1, scores, jnp.full((tok, 1), NEG, F32))

        def gather(j, carry):
            total, acc = carry
            e = jnp.exp2(s_loc[j] - top)
            s_loc[j] = e
            return (total + jnp.sum(e, axis=-1, keepdims=True),
                    acc + dot_nn(e.astype(BF16), vall[j, :, hc]))

        total, acc = lax.fori_loop(0, c + 1, gather, (jnp.zeros((tok, 1), F32), jnp.zeros((tok, HEAD_SIZE), F32)))
        inv = 1.0 / total
        local_out = acc * inv
        delta = jnp.sum(dl * local_out, axis=-1, keepdims=True)

        def back(j, acc):
            dp = dot_nt(dl_low, vall[j, :, hc])
            ds = (s_loc[j] * inv) * (dp - delta)
            return acc + dot_nn(ds.astype(BF16), kall[j, :, hc])

        l_grad[:, hc] = lax.fori_loop(0, c + 1, back, jnp.zeros((tok, HEAD_SIZE), F32))
        l_out[:, hc] = (1.0 - g) * local_out

    def mem_head(h):
        hc = head(h)
        q = q_ref[:, hc]
        g = share_of_gate(h)
        grad = do_ref[:, hc].astype(F32)

        def wait_memory(d):
            p = lax.rem(m + d, n_mem)
            fetched(0, h, p).wait_recv()
            fetched(1, h, p).wait_recv()

        loop(1, n_mem, wait_memory)
        dm = g * grad
        dm_low = dm.astype(BF16)

        def mem_scores(i, top):
            s = dot_nt(q, fk[rows(i * chunk, chunk), hc]) * scale2
            bias = jnp.concatenate(
                [jnp.concatenate([jnp.full((BLOCK, BLOCK), listed(b, 2 * i + x), F32) for x in range(2)], axis=1)
                 for b in range(nqb)], axis=0)
            s = s + bias
            s_mem[i] = s
            return jnp.maximum(top, jnp.max(s, axis=-1, keepdims=True))

        top2 = lax.fori_loop(0, n_chunk, mem_scores, jnp.full((tok, 1), NEG, F32))

        def mem_gather(i, carry):
            total, acc = carry
            e = jnp.exp2(s_mem[i] - top2)
            s_mem[i] = e
            return (total + jnp.sum(e, axis=-1, keepdims=True),
                    acc + dot_nn(e.astype(BF16), fv[rows(i * chunk, chunk), hc]))

        total2, acc2 = lax.fori_loop(0, n_chunk, mem_gather,
                                     (jnp.zeros((tok, 1), F32), jnp.zeros((tok, HEAD_SIZE), F32)))
        inv2 = 1.0 / total2
        mem_out = acc2 * inv2
        m_out[:, hc] = g * mem_out
        delta2 = jnp.sum(dm * mem_out, axis=-1, keepdims=True)

        def mem_back(i, acc):
            dw = dot_nt(dm_low, fv[rows(i * chunk, chunk), hc])
            w = s_mem[i] * inv2
            ds = (w * (dw - delta2)).astype(BF16)
            part_k = (dot_tn(ds, q) * scale).astype(BF16)
            part_v = dot_tn(w.astype(BF16), dm_low).astype(BF16)
            for x in range(2):
                for s in range(nsub):
                    at = slice(x * BLOCK + s * rs, x * BLOCK + (s + 1) * rs)
                    parts[s, 2 * i + x, :, hc] = part_k[at]
                    parts[nsub + s, 2 * i + x, :, hc] = part_v[at]
            return acc + dot_nn(ds, fk[rows(i * chunk, chunk), hc])

        m_grad[:, hc] = lax.fori_loop(0, n_chunk, mem_back, jnp.zeros((tok, HEAD_SIZE), F32))
        loop(1, n_ctx, lambda d: part(h, lax.rem(c + d, n_ctx), c).start())

    def one_head(h):
        @pl.when(h < heads - 1)
        def _():
            local_head(h)

        mem_head(h)

        @pl.when(h > 0)
        def _():
            reduce_head(h - 1)

    loop(0, heads, one_head)
    local_head(heads - 1)
    reduce_head(heads - 1)
    mixed_ref[...] = (m_out[...] + l_out[...]).astype(BF16)
    qg_ref[...] = ((m_grad[...] + l_grad[...]) * scale).astype(BF16)

    def finish(h):
        def arrived(t):
            src_c, i = t // per, lax.rem(t, per)

            @pl.when(jnp.logical_or(src_c != c, c * per + i != m))
            def _():
                owner_copy(h, m, src_c, i, i * width).wait_recv()

        def sent_mem(d):
            p = lax.rem(m + d, n_mem)
            fetch(0, h, p).wait_send()
            fetch(1, h, p).wait_send()
            owner_copy(h, p, c, lax.rem(m, per), col0).wait_send()

        def sent_ctx(p):
            share(0, h, p, c).wait_send()
            share(1, h, p, c).wait_send()

        loop(0, n_ctx * per, arrived)
        loop(1, n_mem, sent_mem)
        loop(c + 1, n_ctx, sent_ctx)
        loop(1, n_ctx, lambda d: part(h, lax.rem(c + d, n_ctx), c).wait_send())

        @pl.when(group != c)
        def _():
            owner_copy(h, m, c, lax.rem(m, per), col0).wait_send()

    loop(0, heads, finish)
    gk_ref[...] = out[0]
    gv_ref[...] = out[1]


def hand_on(a, b, c, d, a_out, b_out, c_out, d_out, sem):
    copies = [
        pltpu.make_async_copy(src, dst, sem.at[i])
        for i, (src, dst) in enumerate(((a, a_out), (b, b_out), (c, c_out), (d, d_out)))
    ]
    for copy in copies:
        copy.start()
    for copy in copies:
        copy.wait()


def shards(n_ctx, n_mem, queries, keys, values, out_grad, mem_keys, mem_values, gate_logit, block_ids):
    tok, width = queries.shape
    columns = mem_keys.shape[1]
    heads = width // HEAD_SIZE
    rs = 2 * BLOCK // n_ctx
    mem_rows = n_mem * BLOCK
    vmem = pl.BlockSpec(memory_space=pltpu.VMEM)
    hbm = pl.BlockSpec(memory_space=pl.ANY)
    dma = pltpu.SemaphoreType.DMA
    pairs = (n_ctx + 1) * tok * tok * heads * HEAD_SIZE
    results = pl.pallas_call(
        functools.partial(kernel, n_ctx, n_mem),
        out_shape=(
            jax.ShapeDtypeStruct((tok, width), BF16),
            jax.ShapeDtypeStruct((tok, width), BF16),
            jax.ShapeDtypeStruct((BLOCK, columns // n_ctx), BF16),
            jax.ShapeDtypeStruct((BLOCK, columns // n_ctx), BF16),
        ),
        in_specs=[hbm] * 8,
        out_specs=(vmem, vmem, vmem, vmem),
        scratch_shapes=[
            pltpu.SMEM(block_ids.shape, jnp.int32),
            pltpu.SMEM(gate_logit.shape, F32),
            pltpu.VMEM((tok, width), BF16),
            pltpu.VMEM((tok, width), BF16),
            pltpu.VMEM((tok, width), F32),
            pltpu.VMEM((tok, width), F32),
            pltpu.VMEM((tok, width), F32),
            pltpu.VMEM((tok, width), F32),
            pltpu.VMEM((n_ctx, tok, width), BF16),
            pltpu.VMEM((n_ctx, tok, width), BF16),
            pltpu.VMEM((mem_rows, width), BF16),
            pltpu.VMEM((mem_rows, width), BF16),
            pltpu.VMEM((n_ctx, n_mem, rs, width), BF16),
            pltpu.VMEM((n_ctx, n_mem, rs, width), BF16),
            pltpu.VMEM((n_mem, rs, width), BF16),
            pltpu.VMEM((2, BLOCK, columns // n_ctx), BF16),
            pltpu.VMEM((n_ctx, tok, tok), F32),
            pltpu.VMEM((mem_rows // (2 * BLOCK), tok, 2 * BLOCK), F32),
            dma((8,)),
            dma((2, heads, n_mem)), dma((2, heads, n_mem)),
            dma((2, heads, n_ctx)), dma((2, heads, n_ctx)),
            dma((heads, n_ctx)), dma((heads, n_ctx)),
            dma((heads, n_mem)), dma((heads, n_ctx, n_mem // n_ctx)),
        ],
        compiler_params=pltpu.CompilerParams(
            collective_id=0, has_side_effects=True, vmem_limit_bytes=62 * 1024 * 1024
        ),
        cost_estimate=pl.CostEstimate(
            flops=8 * pairs, bytes_accessed=8 * 1024 * 1024, transcendentals=4 * tok * tok * heads
        ),
    )(block_ids, gate_logit, queries, keys, values, out_grad, mem_keys, mem_values)
    return pl.pallas_call(
        hand_on,
        out_shape=tuple(jax.ShapeDtypeStruct(r.shape, r.dtype) for r in results),
        in_specs=[hbm] * 4,
        out_specs=(hbm,) * 4,
        scratch_shapes=[dma((4,))],
        compiler_params=pltpu.CompilerParams(vmem_limit_bytes=62 * 1024 * 1024),
    )(*results)


def solution(mesh):
    in_specs = (
        P("ctx", "mem"),
        P("ctx", "mem"),
        P("ctx", "mem"),
        P("ctx", "mem"),
        P("mem", None),
        P("mem", None),
        P("mem"),
        P("ctx", None),
    )
    out_specs = (P("ctx", "mem"), P("ctx", "mem"), P("mem", "ctx"), P("mem", "ctx"))
    body = functools.partial(shards, mesh.shape["ctx"], mesh.shape["mem"])
    return jax.shard_map(body, mesh=mesh, in_specs=in_specs, out_specs=out_specs, check_vma=False)
```

```python
import functools
import math

import jax
import jax.numpy as jnp
from jax import lax
from jax.experimental import pallas as pl
from jax.experimental.pallas import tpu as pltpu
from jax.sharding import PartitionSpec as P

HEAD_SIZE = 128
BLOCK = 128
MESH = pl.DeviceIdType.MESH
UNIT = 16
NEG = -1e30
F32 = jnp.float32
BF16 = jnp.bfloat16


def dot_nt(a, b):
    return lax.dot_general(a, b, (((1,), (1,)), ((), ())), preferred_element_type=F32)


def dot_nn(a, b):
    return lax.dot_general(a, b, (((1,), (0,)), ((), ())), preferred_element_type=F32)


def dot_tn(a, b):
    return lax.dot_general(a, b, (((0,), (0,)), ((), ())), preferred_element_type=F32)


def loop(low, high, body):
    def step(i, carry):
        body(i)
        return carry

    lax.fori_loop(low, high, step, 0)


def kernel(n_ctx, n_mem, ids_in, gate_in, q_in, k_ref, v_ref, do_in, mk_ref, mv_ref,
           mixed_ref, qg_ref, gk_ref, gv_ref,
           ids, gate, q_ref, do_ref, l_out, l_grad, m_out, m_grad, kall, vall, fkv, parts, recv, red, out, s_loc, s_mem,
           own_sem, fsend, frecv, csend, crecv, rsend, rrecv, lsend, lrecv, wsend, psend, precv, osend, orecv):
    c = lax.axis_index("ctx")
    m = lax.axis_index("mem")
    tok, width = q_in.shape
    heads = width // HEAD_SIZE
    nqb = tok // BLOCK
    n_list = ids.shape[1]
    per = n_mem // n_ctx
    nsub = n_ctx // 2
    rs = BLOCK // nsub
    group = m // per
    col0 = lax.rem(m, per) * width
    scale = HEAD_SIZE ** -0.5
    scale2 = scale * math.log2(math.e)
    chunk = 2 * BLOCK
    n_chunk = n_mem * BLOCK // chunk
    unit = UNIT
    direct = BLOCK - nsub * unit
    mine_kv = c // nsub
    mine_row = direct + lax.rem(c, nsub) * unit
    four = n_ctx == 4

    def head(h, base=0):
        return pl.ds(pl.multiple_of(base + h * HEAD_SIZE, HEAD_SIZE), HEAD_SIZE)

    def rows(start, size):
        return pl.ds(pl.multiple_of(start, size), size)

    barrier = pltpu.get_barrier_semaphore()

    def greet(ctx, mem):
        pl.semaphore_signal(barrier, inc=1, device_id={"ctx": ctx, "mem": mem}, device_id_type=MESH)

    loop(1, n_mem, lambda d: greet(c, lax.rem(m + d, n_mem)))
    loop(1, n_ctx, lambda d: greet(lax.rem(c + d, n_ctx), m))

    def greet_owner(t):
        src_c, src_m = t // per, c * per + lax.rem(t, per)

        @pl.when(jnp.logical_or(src_c != c, src_m != m))
        def _():
            greet(src_c, src_m)

    loop(0, n_ctx * per, greet_owner)
    mine = [
        pltpu.make_async_copy(ids_in, ids, own_sem.at[2]),
        pltpu.make_async_copy(gate_in, gate, own_sem.at[3]),
        pltpu.make_async_copy(q_in, q_ref, own_sem.at[4]),
        pltpu.make_async_copy(do_in, do_ref, own_sem.at[5]),
        pltpu.make_async_copy(k_ref, kall.at[c], own_sem.at[6]),
        pltpu.make_async_copy(v_ref, vall.at[c], own_sem.at[7]),
    ]
    if direct:
        mine += [
            pltpu.make_async_copy(src.at[pl.ds(0, direct), rows(m * width, width)],
                                  fkv.at[i, m, pl.ds(0, direct)], own_sem.at[i])
            for i, src in enumerate((mk_ref, mv_ref))
        ]
    for copy in mine:
        copy.start()
    pl.semaphore_wait(barrier, n_mem - 1 + n_ctx - 1 + n_mem - jnp.where(group == c, 1, 0))

    def fetch(which, h, p, slot):
        return pltpu.make_async_remote_copy(
            src_ref=(mk_ref, mv_ref)[which].at[pl.ds(0, direct), head(h, p * width)],
            dst_ref=fkv.at[which, slot, pl.ds(0, direct), head(h)],
            send_sem=fsend.at[which, h, p], recv_sem=frecv.at[which, h, slot],
            device_id={"ctx": c, "mem": p}, device_id_type=MESH)

    def piece(which, p, slot):
        return pltpu.make_async_remote_copy(
            src_ref=(mk_ref, mv_ref)[which].at[rows(mine_row, unit), rows(p * width, width)],
            dst_ref=fkv.at[which, slot, rows(mine_row, unit)],
            send_sem=csend.at[p], recv_sem=crecv.at[slot],
            device_id={"ctx": c, "mem": p}, device_id_type=MESH)

    def own_piece(which):
        return pltpu.make_async_copy(
            (mk_ref, mv_ref)[which].at[rows(mine_row, unit), rows(m * width, width)],
            fkv.at[which, m, rows(mine_row, unit)], own_sem.at[8])

    def relay(p, src):
        at = fkv.at[src // nsub, :, rows(direct + lax.rem(src, nsub) * unit, unit)]
        return pltpu.make_async_remote_copy(
            src_ref=at, dst_ref=at, send_sem=rsend.at[p], recv_sem=rrecv.at[src],
            device_id={"ctx": p, "mem": m}, device_id_type=MESH)

    def both(do):
        for which in range(2):
            pl.when(mine_kv == which)(functools.partial(do, which))

    def forward(which, h, p, slot):
        buf = (kall, vall)[which]
        return pltpu.make_async_remote_copy(
            src_ref=buf.at[slot, :, head(h)], dst_ref=buf.at[slot, :, head(h)],
            send_sem=wsend.at[which, h], recv_sem=lrecv.at[which, h, slot],
            device_id={"ctx": p, "mem": m}, device_id_type=MESH)

    def share(which, h, p, slot):
        src, dst = ((k_ref, kall), (v_ref, vall))[which]
        return pltpu.make_async_remote_copy(
            src_ref=src.at[:, head(h)], dst_ref=dst.at[slot, :, head(h)],
            send_sem=lsend.at[which, h, p], recv_sem=lrecv.at[which, h, slot],
            device_id={"ctx": p, "mem": m}, device_id_type=MESH)

    def part(h, p, slot):
        return pltpu.make_async_remote_copy(
            src_ref=parts.at[p, :, :, head(h)], dst_ref=recv.at[slot, :, :, head(h)],
            send_sem=psend.at[h, p], recv_sem=precv.at[h, slot],
            device_id={"ctx": p, "mem": m}, device_id_type=MESH)

    def owner_copy(h, r, src_c, src_i, base):
        return pltpu.make_async_remote_copy(
            src_ref=red.at[r, :, head(h)],
            dst_ref=out.at[src_c // nsub, rows(lax.rem(src_c, nsub) * rs, rs), head(h, base)],
            send_sem=osend.at[h, r], recv_sem=orecv.at[h, src_c, src_i],
            device_id={"ctx": group, "mem": r}, device_id_type=MESH)

    def apart(p):
        return c + p != 3 if four else p >= 0

    def start_share(h):
        def to_ctx(p):
            @pl.when(apart(p))
            def _():
                share(0, h, p, c).start()
                share(1, h, p, c).start()

        loop(c + 1, n_ctx, to_ctx)

    def start_fetch(h):
        def to_mem(d):
            p = lax.rem(m + d, n_mem)
            fetch(0, h, p, m).start()
            fetch(1, h, p, m).start()

        loop(1, n_mem, to_mem)

    def send_pieces(which):
        own_piece(which).start()
        loop(1, n_mem, lambda d: piece(which, lax.rem(m + d, n_mem), m).start())

    def take_pieces(which):
        own_piece(which).wait()

        def take(d):
            p = lax.rem(m + d, n_mem)
            piece(which, p, p).wait_recv()

        loop(1, n_mem, take)

    both(send_pieces)
    start_share(0)
    if direct:
        loop(0, heads, start_fetch)
    for copy in mine:
        copy.wait()
    both(take_pieces)
    loop(1, n_ctx, lambda d: relay(lax.rem(c + d, n_ctx), c).start())
    loop(1, heads, start_share)

    def pass_on(h):
        if four:
            for at, which, slot, to in ((1, 0, 0, 3), (2, 1, 0, 3), (3, 0, 1, 2), (3, 1, 1, 2)):
                @pl.when(c == at)
                def _(which=which, slot=slot, to=to):
                    share(which, h, slot, slot).wait_recv()
                    forward(which, h, to, slot).start()

    difference = (lax.broadcasted_iota(jnp.int32, (tok, tok), 1)
                  - lax.broadcasted_iota(jnp.int32, (tok, tok), 0))

    def listed(b, r):
        hit = ids[b, 0] == r
        for j in range(1, n_list):
            hit = jnp.logical_or(hit, ids[b, j] == r)
        return jnp.where(hit, 0.0, NEG).astype(F32)

    def reduce_head(h):
        total = parts[c, :, :, head(h)].astype(F32)

        def add(d, total):
            src = lax.rem(c + d, n_ctx)
            part(h, src, src).wait_recv()
            return total + recv[src, :, :, head(h)].astype(F32)

        total = lax.fori_loop(1, n_ctx, add, total)
        red[:, :, head(h)] = total.astype(BF16)

        def send(d):
            r = lax.rem(m + d, n_mem)
            owner_copy(h, r, c, lax.rem(m, per), col0).start()

        loop(1, n_mem, send)

        @pl.when(group == c)
        def _():
            out[c // nsub, rows(lax.rem(c, nsub) * rs, rs), head(h, col0)] = red[m, :, head(h)]

        @pl.when(group != c)
        def _():
            owner_copy(h, m, c, lax.rem(m, per), col0).start()

    def share_of_gate(h):
        return 1.0 / (1.0 + jnp.exp(-jnp.full((1, HEAD_SIZE), gate[h], F32)))

    def local_head(h):
        hc = head(h)
        q = q_ref[:, hc]
        g = share_of_gate(h)
        grad = do_ref[:, hc].astype(F32)
        dl = (1.0 - g) * grad
        dl_low = dl.astype(BF16)

        def wait_local(j):
            for which in range(2):
                if four:
                    ahead = jnp.logical_or(jnp.logical_and(c == 1 + which, j == 0), jnp.logical_and(c == 3, j == 1))
                    pl.when(jnp.logical_not(ahead))(lambda: share(which, h, j, j).wait_recv())
                else:
                    share(which, h, j, j).wait_recv()

        loop(0, c, wait_local)

        def scores(j, top):
            s = dot_nt(q, kall[j, :, hc]) * scale2
            s = jnp.where(difference <= (c - j) * tok, s, NEG)
            s_loc[j] = s
            return jnp.maximum(top, jnp.max(s, axis=-1, keepdims=True))

        top = lax.fori_loop(0, c + 1, scores, jnp.full((tok, 1), NEG, F32))

        def gather(j, carry):
            total, acc = carry
            e = jnp.exp2(s_loc[j] - top)
            s_loc[j] = e
            return (total + jnp.sum(e, axis=-1, keepdims=True),
                    acc + dot_nn(e.astype(BF16), vall[j, :, hc]))

        total, acc = lax.fori_loop(0, c + 1, gather, (jnp.zeros((tok, 1), F32), jnp.zeros((tok, HEAD_SIZE), F32)))
        inv = 1.0 / total
        local_out = acc * inv
        delta = jnp.sum(dl * local_out, axis=-1, keepdims=True)

        def back(j, acc):
            dp = dot_nt(dl_low, vall[j, :, hc])
            ds = (s_loc[j] * inv) * (dp - delta)
            return acc + dot_nn(ds.astype(BF16), kall[j, :, hc])

        l_grad[:, hc] = lax.fori_loop(0, c + 1, back, jnp.zeros((tok, HEAD_SIZE), F32))
        l_out[:, hc] = (1.0 - g) * local_out

    def mem_head(h):
        hc = head(h)
        q = q_ref[:, hc]
        g = share_of_gate(h)
        grad = do_ref[:, hc].astype(F32)

        def wait_memory(d):
            p = lax.rem(m + d, n_mem)
            fetch(0, h, p, p).wait_recv()
            fetch(1, h, p, p).wait_recv()

        if direct:
            loop(1, n_mem, wait_memory)

        @pl.when(h == 0)
        def _():
            def wait_relay(d):
                src = lax.rem(c + d, n_ctx)
                relay(src, src).wait_recv()

            loop(1, n_ctx, wait_relay)

        def rows_of(which, i):
            return jnp.concatenate([fkv[which, 2 * i + x, :, hc] for x in range(2)], axis=0)

        unroll = math.gcd(n_chunk, 4)
        dm = g * grad
        dm_low = dm.astype(BF16)

        def mem_scores(i, top):
            s = dot_nt(q, rows_of(0, i)) * scale2
            bias = jnp.concatenate(
                [jnp.concatenate([jnp.full((BLOCK, BLOCK), listed(b, 2 * i + x), F32) for x in range(2)], axis=1)
                 for b in range(nqb)], axis=0)
            s = s + bias
            s_mem[i] = s
            return jnp.maximum(top, jnp.max(s, axis=-1, keepdims=True))

        top2 = lax.fori_loop(0, n_chunk, mem_scores, jnp.full((tok, 1), NEG, F32), unroll=unroll)

        def mem_gather(i, carry):
            total, acc = carry
            e = jnp.exp2(s_mem[i] - top2)
            s_mem[i] = e
            return (total + jnp.sum(e, axis=-1, keepdims=True),
                    acc + dot_nn(e.astype(BF16), rows_of(1, i)))

        total2, acc2 = lax.fori_loop(0, n_chunk, mem_gather,
                                     (jnp.zeros((tok, 1), F32), jnp.zeros((tok, HEAD_SIZE), F32)), unroll=unroll)
        inv2 = 1.0 / total2
        mem_out = acc2 * inv2
        m_out[:, hc] = g * mem_out
        delta2 = jnp.sum(dm * mem_out, axis=-1, keepdims=True)

        def mem_back(i, acc):
            dw = dot_nt(dm_low, rows_of(1, i))
            w = s_mem[i] * inv2
            ds = (w * (dw - delta2)).astype(BF16)
            part_k = (dot_tn(ds, q) * scale).astype(BF16)
            part_v = dot_tn(w.astype(BF16), dm_low).astype(BF16)
            for x in range(2):
                for s in range(nsub):
                    at = slice(x * BLOCK + s * rs, x * BLOCK + (s + 1) * rs)
                    parts[s, 2 * i + x, :, hc] = part_k[at]
                    parts[nsub + s, 2 * i + x, :, hc] = part_v[at]
            return acc + dot_nn(ds, rows_of(0, i))

        m_grad[:, hc] = lax.fori_loop(0, n_chunk, mem_back, jnp.zeros((tok, HEAD_SIZE), F32), unroll=unroll)
        loop(1, n_ctx, lambda d: part(h, lax.rem(c + d, n_ctx), c).start())

    def one_head(h):
        @pl.when(h < heads - 1)
        def _():
            local_head(h)

        @pl.when(h < heads - 1)
        def _():
            pass_on(h + 1)

        mem_head(h)

        @pl.when(h > 0)
        def _():
            reduce_head(h - 1)

    pass_on(0)
    loop(0, heads, one_head)
    local_head(heads - 1)
    reduce_head(heads - 1)
    mixed_ref[...] = (m_out[...] + l_out[...]).astype(BF16)
    qg_ref[...] = ((m_grad[...] + l_grad[...]) * scale).astype(BF16)

    def finish(h):
        def arrived(t):
            src_c, i = t // per, lax.rem(t, per)

            @pl.when(jnp.logical_or(src_c != c, c * per + i != m))
            def _():
                owner_copy(h, m, src_c, i, i * width).wait_recv()

        def sent_mem(d):
            p = lax.rem(m + d, n_mem)
            if direct:
                fetch(0, h, p, m).wait_send()
                fetch(1, h, p, m).wait_send()
            owner_copy(h, p, c, lax.rem(m, per), col0).wait_send()

        def sent_ctx(p):
            @pl.when(apart(p))
            def _():
                share(0, h, p, c).wait_send()
                share(1, h, p, c).wait_send()

        if four:
            for at, which, slot, to in ((1, 0, 0, 3), (2, 1, 0, 3), (3, 0, 1, 2), (3, 1, 1, 2)):
                pl.when(c == at)(forward(which, h, to, slot).wait_send)

        loop(0, n_ctx * per, arrived)
        loop(1, n_mem, sent_mem)
        loop(c + 1, n_ctx, sent_ctx)
        loop(1, n_ctx, lambda d: part(h, lax.rem(c + d, n_ctx), c).wait_send())

        @pl.when(group != c)
        def _():
            owner_copy(h, m, c, lax.rem(m, per), col0).wait_send()

    loop(0, heads, finish)
    both(lambda which: loop(1, n_mem, lambda d: piece(which, lax.rem(m + d, n_mem), m).wait_send()))
    loop(1, n_ctx, lambda d: relay(lax.rem(c + d, n_ctx), c).wait_send())
    gk_ref[...] = out[0]
    gv_ref[...] = out[1]


def hand_on(*refs):
    for src, dst in zip(refs[:4], refs[4:]):
        dst[...] = src[...]


def shards(n_ctx, n_mem, queries, keys, values, out_grad, mem_keys, mem_values, gate_logit, block_ids):
    tok, width = queries.shape
    columns = mem_keys.shape[1]
    heads = width // HEAD_SIZE
    rs = 2 * BLOCK // n_ctx
    mem_rows = n_mem * BLOCK
    vmem = pl.BlockSpec(memory_space=pltpu.VMEM)
    hbm = pl.BlockSpec(memory_space=pl.ANY)
    dma = pltpu.SemaphoreType.DMA
    pairs = (n_ctx + 1) * tok * tok * heads * HEAD_SIZE
    results = pl.pallas_call(
        functools.partial(kernel, n_ctx, n_mem),
        out_shape=(
            jax.ShapeDtypeStruct((tok, width), BF16),
            jax.ShapeDtypeStruct((tok, width), BF16),
            jax.ShapeDtypeStruct((BLOCK, columns // n_ctx), BF16),
            jax.ShapeDtypeStruct((BLOCK, columns // n_ctx), BF16),
        ),
        in_specs=[hbm] * 8,
        out_specs=(vmem, vmem, vmem, vmem),
        scratch_shapes=[
            pltpu.SMEM(block_ids.shape, jnp.int32),
            pltpu.SMEM(gate_logit.shape, F32),
            pltpu.VMEM((tok, width), BF16),
            pltpu.VMEM((tok, width), BF16),
            pltpu.VMEM((tok, width), F32),
            pltpu.VMEM((tok, width), F32),
            pltpu.VMEM((tok, width), F32),
            pltpu.VMEM((tok, width), F32),
            pltpu.VMEM((n_ctx, tok, width), BF16),
            pltpu.VMEM((n_ctx, tok, width), BF16),
            pltpu.VMEM((2, n_mem, BLOCK, width), BF16),
            pltpu.VMEM((n_ctx, n_mem, rs, width), BF16),
            pltpu.VMEM((n_ctx, n_mem, rs, width), BF16),
            pltpu.VMEM((n_mem, rs, width), BF16),
            pltpu.VMEM((2, BLOCK, columns // n_ctx), BF16),
            pltpu.VMEM((n_ctx, tok, tok), F32),
            pltpu.VMEM((mem_rows // (2 * BLOCK), tok, 2 * BLOCK), F32),
            dma((9,)),
            dma((2, heads, n_mem)), dma((2, heads, n_mem)),
            dma((n_mem,)), dma((n_mem,)),
            dma((n_ctx,)), dma((n_ctx,)),
            dma((2, heads, n_ctx)), dma((2, heads, n_ctx)), dma((2, heads)),
            dma((heads, n_ctx)), dma((heads, n_ctx)),
            dma((heads, n_mem)), dma((heads, n_ctx, n_mem // n_ctx)),
        ],
        compiler_params=pltpu.CompilerParams(
            collective_id=0, has_side_effects=True, vmem_limit_bytes=62 * 1024 * 1024
        ),
        cost_estimate=pl.CostEstimate(
            flops=8 * pairs, bytes_accessed=8 * 1024 * 1024, transcendentals=4 * tok * tok * heads
        ),
    )(block_ids, gate_logit, queries, keys, values, out_grad, mem_keys, mem_values)
    return pl.pallas_call(
        hand_on,
        out_shape=tuple(jax.ShapeDtypeStruct(r.shape, r.dtype) for r in results),
        in_specs=[vmem] * 4,
        out_specs=(vmem,) * 4,
    )(*results)


def solution(mesh):
    in_specs = (
        P("ctx", "mem"),
        P("ctx", "mem"),
        P("ctx", "mem"),
        P("ctx", "mem"),
        P("mem", None),
        P("mem", None),
        P("mem"),
        P("ctx", None),
    )
    out_specs = (P("ctx", "mem"), P("ctx", "mem"), P("mem", "ctx"), P("mem", "ctx"))
    body = functools.partial(shards, mesh.shape["ctx"], mesh.shape["mem"])
    return jax.shard_map(body, mesh=mesh, in_specs=in_specs, out_specs=out_specs, check_vma=False)
```

```python
import functools
import math

import jax
import jax.numpy as jnp
from jax import lax
from jax.experimental import pallas as pl
from jax.experimental.pallas import tpu as pltpu
from jax.sharding import PartitionSpec as P

HEAD_SIZE = 128
BLOCK = 128
MESH = pl.DeviceIdType.MESH
NEG = -1e30
F32 = jnp.float32
BF16 = jnp.bfloat16


def dot_nt(a, b):
    return lax.dot_general(a, b, (((1,), (1,)), ((), ())), preferred_element_type=F32)


def dot_nn(a, b):
    return lax.dot_general(a, b, (((1,), (0,)), ((), ())), preferred_element_type=F32)


def dot_tn(a, b):
    return lax.dot_general(a, b, (((0,), (0,)), ((), ())), preferred_element_type=F32)


def loop(low, high, body):
    def step(i, carry):
        body(i)
        return carry

    lax.fori_loop(low, high, step, 0)


def kernel(n_ctx, n_mem, ids_in, gate_in, q_in, k_ref, v_ref, do_in, mk_ref, mv_ref,
           mixed_ref, qg_ref, gk_ref, gv_ref,
           ids, gate, q_ref, do_ref, l_out, l_grad, m_out, m_grad, kall, vall, fk, fv, parts, recv, red, out, s_loc, s_mem,
           own_sem, fsend, frecv, lsend, lrecv, psend, precv, osend, orecv):
    c = lax.axis_index("ctx")
    m = lax.axis_index("mem")
    tok, width = q_in.shape
    heads = width // HEAD_SIZE
    nqb = tok // BLOCK
    n_list = ids.shape[1]
    per = n_mem // n_ctx
    nsub = n_ctx // 2
    rs = BLOCK // nsub
    group = m // per
    col0 = lax.rem(m, per) * width
    scale = HEAD_SIZE ** -0.5
    scale2 = scale * math.log2(math.e)
    chunk = 2 * BLOCK
    n_chunk = n_mem * BLOCK // chunk

    def head(h, base=0):
        return pl.ds(pl.multiple_of(base + h * HEAD_SIZE, HEAD_SIZE), HEAD_SIZE)

    def rows(start, size):
        return pl.ds(pl.multiple_of(start, size), size)

    barrier = pltpu.get_barrier_semaphore()

    def greet(ctx, mem):
        pl.semaphore_signal(barrier, inc=1, device_id={"ctx": ctx, "mem": mem}, device_id_type=MESH)

    loop(1, n_mem, lambda d: greet(c, lax.rem(m + d, n_mem)))
    loop(1, n_ctx, lambda d: greet(lax.rem(c + d, n_ctx), m))

    def greet_owner(t):
        src_c, src_m = t // per, c * per + lax.rem(t, per)

        @pl.when(jnp.logical_or(src_c != c, src_m != m))
        def _():
            greet(src_c, src_m)

    loop(0, n_ctx * per, greet_owner)
    own_k = pltpu.make_async_copy(mk_ref.at[:, rows(m * width, width)], fk.at[rows(m * BLOCK, BLOCK)], own_sem.at[0])
    own_v = pltpu.make_async_copy(mv_ref.at[:, rows(m * width, width)], fv.at[rows(m * BLOCK, BLOCK)], own_sem.at[1])
    mine = [
        pltpu.make_async_copy(ids_in, ids, own_sem.at[2]),
        pltpu.make_async_copy(gate_in, gate, own_sem.at[3]),
        pltpu.make_async_copy(q_in, q_ref, own_sem.at[4]),
        pltpu.make_async_copy(do_in, do_ref, own_sem.at[5]),
        pltpu.make_async_copy(k_ref, kall.at[c], own_sem.at[6]),
        pltpu.make_async_copy(v_ref, vall.at[c], own_sem.at[7]),
        own_k,
        own_v,
    ]
    for copy in mine:
        copy.start()
    pl.semaphore_wait(barrier, n_mem - 1 + n_ctx - 1 + n_mem - jnp.where(group == c, 1, 0))

    def fetch(which, h, p):
        src, dst = ((mk_ref, fk), (mv_ref, fv))[which]
        return pltpu.make_async_remote_copy(
            src_ref=src.at[:, head(h, p * width)], dst_ref=dst.at[rows(m * BLOCK, BLOCK), head(h)],
            send_sem=fsend.at[which, h, p], recv_sem=frecv.at[which, h, m],
            device_id={"ctx": c, "mem": p}, device_id_type=MESH)

    def fetched(which, h, p):
        src, dst = ((mk_ref, fk), (mv_ref, fv))[which]
        return pltpu.make_async_remote_copy(
            src_ref=src.at[:, head(h, p * width)], dst_ref=dst.at[rows(p * BLOCK, BLOCK), head(h)],
            send_sem=fsend.at[which, h, p], recv_sem=frecv.at[which, h, p],
            device_id={"ctx": c, "mem": p}, device_id_type=MESH)

    def share(which, h, p, slot):
        src, dst = ((k_ref, kall), (v_ref, vall))[which]
        return pltpu.make_async_remote_copy(
            src_ref=src.at[:, head(h)], dst_ref=dst.at[slot, :, head(h)],
            send_sem=lsend.at[which, h, p], recv_sem=lrecv.at[which, h, slot],
            device_id={"ctx": p, "mem": m}, device_id_type=MESH)

    def part(h, p, slot):
        return pltpu.make_async_remote_copy(
            src_ref=parts.at[p, :, :, head(h)], dst_ref=recv.at[slot, :, :, head(h)],
            send_sem=psend.at[h, p], recv_sem=precv.at[h, slot],
            device_id={"ctx": p, "mem": m}, device_id_type=MESH)

    def owner_copy(h, r, src_c, src_i, base):
        return pltpu.make_async_remote_copy(
            src_ref=red.at[r, :, head(h)],
            dst_ref=out.at[src_c // nsub, rows(lax.rem(src_c, nsub) * rs, rs), head(h, base)],
            send_sem=osend.at[h, r], recv_sem=orecv.at[h, src_c, src_i],
            device_id={"ctx": group, "mem": r}, device_id_type=MESH)

    def start_head(h):
        def to_mem(d):
            p = lax.rem(m + d, n_mem)
            fetch(0, h, p).start()
            fetch(1, h, p).start()

        def to_ctx(p):
            share(0, h, p, c).start()
            share(1, h, p, c).start()

        loop(c + 1, n_ctx, to_ctx)
        loop(1, n_mem, to_mem)

    loop(0, heads, start_head)
    for copy in mine:
        copy.wait()

    causal = (lax.broadcasted_iota(jnp.int32, (tok, tok), 0)
              <= lax.broadcasted_iota(jnp.int32, (tok, tok), 1))

    def listed(b, r):
        hit = ids[b, 0] == r
        for j in range(1, n_list):
            hit = jnp.logical_or(hit, ids[b, j] == r)
        return jnp.where(hit, 0.0, NEG).astype(F32)

    def reduce_head(h):
        total = parts[c, :, :, head(h)].astype(F32)

        def add(d, total):
            src = lax.rem(c + d, n_ctx)
            part(h, src, src).wait_recv()
            return total + recv[src, :, :, head(h)].astype(F32)

        total = lax.fori_loop(1, n_ctx, add, total)
        red[:, :, head(h)] = total.astype(BF16)

        def send(d):
            r = lax.rem(m + d, n_mem)
            owner_copy(h, r, c, lax.rem(m, per), col0).start()

        loop(1, n_mem, send)

        @pl.when(group == c)
        def _():
            out[c // nsub, rows(lax.rem(c, nsub) * rs, rs), head(h, col0)] = red[m, :, head(h)]

        @pl.when(group != c)
        def _():
            owner_copy(h, m, c, lax.rem(m, per), col0).start()

    def share_of_gate(h):
        return 1.0 / (1.0 + jnp.exp(-jnp.full((1, HEAD_SIZE), gate[h], F32)))

    def row_max(s):
        return jnp.max(s, axis=0, keepdims=True)

    def row_sum(s):
        return jnp.sum(s, axis=0, keepdims=True)

    def gradient(h, share):
        return (share * do_ref[:, head(h)].astype(F32))

    def local_head(h):
        hc = head(h)
        q = q_ref[:, hc]
        keep = 1.0 - share_of_gate(h)
        dl = gradient(h, keep)
        dl_low = dl.astype(BF16)
        dl_t = dl.T

        def wait_local(j):
            share(0, h, j, j).wait_recv()
            share(1, h, j, j).wait_recv()

        loop(0, c, wait_local)

        s = jnp.where(causal, dot_nt(kall[c, :, hc], q) * scale2, NEG)
        s_loc[c] = s

        def scores(j, top):
            s = dot_nt(kall[j, :, hc], q) * scale2
            s_loc[j] = s
            return jnp.maximum(top, row_max(s))

        top = lax.fori_loop(0, c, scores, row_max(s))

        def gather(j, carry):
            total, acc = carry
            e = jnp.exp2(s_loc[j] - top)
            s_loc[j] = e
            return total + row_sum(e), acc + dot_tn(vall[j, :, hc], e.astype(BF16))

        total, acc = lax.fori_loop(0, c + 1, gather, (jnp.zeros((1, tok), F32), jnp.zeros((HEAD_SIZE, tok), F32)))
        inv = 1.0 / total
        local_out = acc * inv
        delta = row_sum(dl_t * local_out)

        def back(j, acc):
            dp = dot_nt(vall[j, :, hc], dl_low)
            ds = (s_loc[j] * inv) * (dp - delta)
            return acc + dot_tn(kall[j, :, hc], ds.astype(BF16))

        l_grad[rows(h * HEAD_SIZE, HEAD_SIZE), :] = lax.fori_loop(0, c + 1, back, jnp.zeros((HEAD_SIZE, tok), F32))
        l_out[rows(h * HEAD_SIZE, HEAD_SIZE), :] = keep[:, :1] * local_out

    def mem_head(h):
        hc = head(h)
        q = q_ref[:, hc]
        g = share_of_gate(h)
        dm = gradient(h, g)
        dm_low = dm.astype(BF16)
        dm_t = dm.T

        def wait_memory(d):
            p = lax.rem(m + d, n_mem)
            fetched(0, h, p).wait_recv()
            fetched(1, h, p).wait_recv()

        loop(1, n_mem, wait_memory)

        def mem_scores(i, top):
            s = dot_nt(fk[rows(i * chunk, chunk), hc], q) * scale2
            bias = [jnp.concatenate([jnp.full((1, BLOCK), listed(b, 2 * i + x), F32) for b in range(nqb)], axis=1)
                    for x in range(2)]
            s = jnp.concatenate([s[:BLOCK] + bias[0], s[BLOCK:] + bias[1]], axis=0)
            s_mem[i] = s
            return jnp.maximum(top, row_max(s))

        top = lax.fori_loop(0, n_chunk, mem_scores, jnp.full((1, tok), NEG, F32))

        def mem_gather(i, carry):
            total, acc = carry
            e = jnp.exp2(s_mem[i] - top)
            s_mem[i] = e
            return total + row_sum(e), acc + dot_tn(fv[rows(i * chunk, chunk), hc], e.astype(BF16))

        total, acc = lax.fori_loop(0, n_chunk, mem_gather,
                                   (jnp.zeros((1, tok), F32), jnp.zeros((HEAD_SIZE, tok), F32)))
        inv = 1.0 / total
        mem_out = acc * inv
        m_out[rows(h * HEAD_SIZE, HEAD_SIZE), :] = g[:, :1] * mem_out
        delta = row_sum(dm_t * mem_out)

        def mem_back(i, acc):
            dw = dot_nt(fv[rows(i * chunk, chunk), hc], dm_low)
            w = s_mem[i] * inv
            ds = (w * (dw - delta)).astype(BF16)
            part_k = (dot_nn(ds, q) * scale).astype(BF16)
            part_v = dot_nn(w.astype(BF16), dm_low).astype(BF16)
            for x in range(2):
                for s in range(nsub):
                    at = slice(x * BLOCK + s * rs, x * BLOCK + (s + 1) * rs)
                    parts[s, 2 * i + x, :, hc] = part_k[at]
                    parts[nsub + s, 2 * i + x, :, hc] = part_v[at]
            return acc + dot_tn(fk[rows(i * chunk, chunk), hc], ds)

        m_grad[rows(h * HEAD_SIZE, HEAD_SIZE), :] = lax.fori_loop(0, n_chunk, mem_back, jnp.zeros((HEAD_SIZE, tok), F32))
        loop(1, n_ctx, lambda d: part(h, lax.rem(c + d, n_ctx), c).start())

    def one_head(h):
        @pl.when(h < heads - 1)
        def _():
            local_head(h)

        mem_head(h)

        @pl.when(h > 0)
        def _():
            reduce_head(h - 1)

    loop(0, heads, one_head)
    local_head(heads - 1)
    reduce_head(heads - 1)
    mixed_ref[...] = (m_out[...] + l_out[...]).T.astype(BF16)
    qg_ref[...] = ((m_grad[...] + l_grad[...]) * scale).T.astype(BF16)

    def finish(h):
        def arrived(t):
            src_c, i = t // per, lax.rem(t, per)

            @pl.when(jnp.logical_or(src_c != c, c * per + i != m))
            def _():
                owner_copy(h, m, src_c, i, i * width).wait_recv()

        def sent_mem(d):
            p = lax.rem(m + d, n_mem)
            fetch(0, h, p).wait_send()
            fetch(1, h, p).wait_send()
            owner_copy(h, p, c, lax.rem(m, per), col0).wait_send()

        def sent_ctx(p):
            share(0, h, p, c).wait_send()
            share(1, h, p, c).wait_send()

        loop(0, n_ctx * per, arrived)
        loop(1, n_mem, sent_mem)
        loop(c + 1, n_ctx, sent_ctx)
        loop(1, n_ctx, lambda d: part(h, lax.rem(c + d, n_ctx), c).wait_send())

        @pl.when(group != c)
        def _():
            owner_copy(h, m, c, lax.rem(m, per), col0).wait_send()

    loop(0, heads, finish)
    gk_ref[...] = out[0]
    gv_ref[...] = out[1]


def hand_on(*refs):
    for src, dst in zip(refs[:4], refs[4:]):
        dst[...] = src[...]


def shards(n_ctx, n_mem, queries, keys, values, out_grad, mem_keys, mem_values, gate_logit, block_ids):
    tok, width = queries.shape
    columns = mem_keys.shape[1]
    heads = width // HEAD_SIZE
    rs = 2 * BLOCK // n_ctx
    mem_rows = n_mem * BLOCK
    vmem = pl.BlockSpec(memory_space=pltpu.VMEM)
    hbm = pl.BlockSpec(memory_space=pl.ANY)
    dma = pltpu.SemaphoreType.DMA
    pairs = (n_ctx + 1) * tok * tok * heads * HEAD_SIZE
    results = pl.pallas_call(
        functools.partial(kernel, n_ctx, n_mem),
        out_shape=(
            jax.ShapeDtypeStruct((tok, width), BF16),
            jax.ShapeDtypeStruct((tok, width), BF16),
            jax.ShapeDtypeStruct((BLOCK, columns // n_ctx), BF16),
            jax.ShapeDtypeStruct((BLOCK, columns // n_ctx), BF16),
        ),
        in_specs=[hbm] * 8,
        out_specs=(vmem, vmem, vmem, vmem),
        scratch_shapes=[
            pltpu.SMEM(block_ids.shape, jnp.int32),
            pltpu.SMEM(gate_logit.shape, F32),
            pltpu.VMEM((tok, width), BF16),
            pltpu.VMEM((tok, width), BF16),
            pltpu.VMEM((width, tok), F32),
            pltpu.VMEM((width, tok), F32),
            pltpu.VMEM((width, tok), F32),
            pltpu.VMEM((width, tok), F32),
            pltpu.VMEM((n_ctx, tok, width), BF16),
            pltpu.VMEM((n_ctx, tok, width), BF16),
            pltpu.VMEM((mem_rows, width), BF16),
            pltpu.VMEM((mem_rows, width), BF16),
            pltpu.VMEM((n_ctx, n_mem, rs, width), BF16),
            pltpu.VMEM((n_ctx, n_mem, rs, width), BF16),
            pltpu.VMEM((n_mem, rs, width), BF16),
            pltpu.VMEM((2, BLOCK, columns // n_ctx), BF16),
            pltpu.VMEM((n_ctx, tok, tok), F32),
            pltpu.VMEM((mem_rows // (2 * BLOCK), 2 * BLOCK, tok), F32),
            dma((8,)),
            dma((2, heads, n_mem)), dma((2, heads, n_mem)),
            dma((2, heads, n_ctx)), dma((2, heads, n_ctx)),
            dma((heads, n_ctx)), dma((heads, n_ctx)),
            dma((heads, n_mem)), dma((heads, n_ctx, n_mem // n_ctx)),
        ],
        compiler_params=pltpu.CompilerParams(
            collective_id=0, has_side_effects=True, vmem_limit_bytes=62 * 1024 * 1024
        ),
        cost_estimate=pl.CostEstimate(
            flops=8 * pairs, bytes_accessed=8 * 1024 * 1024, transcendentals=4 * tok * tok * heads
        ),
    )(block_ids, gate_logit, queries, keys, values, out_grad, mem_keys, mem_values)
    return pl.pallas_call(
        hand_on,
        out_shape=tuple(jax.ShapeDtypeStruct(r.shape, r.dtype) for r in results),
        in_specs=[vmem] * 4,
        out_specs=(vmem,) * 4,
    )(*results)


def solution(mesh):
    in_specs = (
        P("ctx", "mem"),
        P("ctx", "mem"),
        P("ctx", "mem"),
        P("ctx", "mem"),
        P("mem", None),
        P("mem", None),
        P("mem"),
        P("ctx", None),
    )
    out_specs = (P("ctx", "mem"), P("ctx", "mem"), P("mem", "ctx"), P("mem", "ctx"))
    body = functools.partial(shards, mesh.shape["ctx"], mesh.shape["mem"])
    return jax.shard_map(body, mesh=mesh, in_specs=in_specs, out_specs=out_specs, check_vma=False)
```

```python
import functools
import math

import jax
import jax.numpy as jnp
from jax import lax
from jax.experimental import pallas as pl
from jax.experimental.pallas import tpu as pltpu
from jax.sharding import PartitionSpec as P

HEAD_SIZE = 128
BLOCK = 128
MESH = pl.DeviceIdType.MESH
NEG = -1e30
F32 = jnp.float32
BF16 = jnp.bfloat16


def dot_nt(a, b):
    return lax.dot_general(a, b, (((1,), (1,)), ((), ())), preferred_element_type=F32)


def dot_nn(a, b):
    return lax.dot_general(a, b, (((1,), (0,)), ((), ())), preferred_element_type=F32)


def dot_tn(a, b):
    return lax.dot_general(a, b, (((0,), (0,)), ((), ())), preferred_element_type=F32)


def loop(low, high, body):
    def step(i, carry):
        body(i)
        return carry

    lax.fori_loop(low, high, step, 0)


def kernel(n_ctx, n_mem, ids_in, gate_in, q_in, k_ref, v_ref, do_in, mk_ref, mv_ref,
           mixed_ref, qg_ref, gk_ref, gv_ref,
           ids, gate, q_ref, do_ref, l_out, l_grad, m_out, m_grad, kall, vall, fk, fv, parts, recv, red, out, s_loc, s_mem,
           own_sem, fsend, frecv, lsend, lrecv, wsend, psend, precv, osend, orecv):
    c = lax.axis_index("ctx")
    m = lax.axis_index("mem")
    tok, width = q_in.shape
    heads = width // HEAD_SIZE
    nqb = tok // BLOCK
    n_list = ids.shape[1]
    per = n_mem // n_ctx
    nsub = n_ctx // 2
    rs = BLOCK // nsub
    group = m // per
    col0 = lax.rem(m, per) * width
    scale = HEAD_SIZE ** -0.5
    scale2 = scale * math.log2(math.e)
    chunk = 2 * BLOCK
    n_chunk = n_mem * BLOCK // chunk
    four = n_ctx == 4

    def head(h, base=0):
        return pl.ds(pl.multiple_of(base + h * HEAD_SIZE, HEAD_SIZE), HEAD_SIZE)

    def rows(start, size):
        return pl.ds(pl.multiple_of(start, size), size)

    barrier = pltpu.get_barrier_semaphore()

    def greet(ctx, mem):
        pl.semaphore_signal(barrier, inc=1, device_id={"ctx": ctx, "mem": mem}, device_id_type=MESH)

    loop(1, n_mem, lambda d: greet(c, lax.rem(m + d, n_mem)))
    loop(1, n_ctx, lambda d: greet(lax.rem(c + d, n_ctx), m))

    def greet_owner(t):
        src_c, src_m = t // per, c * per + lax.rem(t, per)

        @pl.when(jnp.logical_or(src_c != c, src_m != m))
        def _():
            greet(src_c, src_m)

    loop(0, n_ctx * per, greet_owner)
    own_k = pltpu.make_async_copy(mk_ref.at[:, rows(m * width, width)], fk.at[rows(m * BLOCK, BLOCK)], own_sem.at[0])
    own_v = pltpu.make_async_copy(mv_ref.at[:, rows(m * width, width)], fv.at[rows(m * BLOCK, BLOCK)], own_sem.at[1])
    mine = [
        pltpu.make_async_copy(ids_in, ids, own_sem.at[2]),
        pltpu.make_async_copy(gate_in, gate, own_sem.at[3]),
        pltpu.make_async_copy(q_in, q_ref, own_sem.at[4]),
        pltpu.make_async_copy(do_in, do_ref, own_sem.at[5]),
        pltpu.make_async_copy(k_ref, kall.at[c], own_sem.at[6]),
        pltpu.make_async_copy(v_ref, vall.at[c], own_sem.at[7]),
        own_k,
        own_v,
    ]
    for copy in mine:
        copy.start()
    pl.semaphore_wait(barrier, n_mem - 1 + n_ctx - 1 + n_mem - jnp.where(group == c, 1, 0))

    def fetch(which, h, p):
        src, dst = ((mk_ref, fk), (mv_ref, fv))[which]
        return pltpu.make_async_remote_copy(
            src_ref=src.at[:, head(h, p * width)], dst_ref=dst.at[rows(m * BLOCK, BLOCK), head(h)],
            send_sem=fsend.at[which, h, p], recv_sem=frecv.at[which, h, m],
            device_id={"ctx": c, "mem": p}, device_id_type=MESH)

    def fetched(which, h, p):
        src, dst = ((mk_ref, fk), (mv_ref, fv))[which]
        return pltpu.make_async_remote_copy(
            src_ref=src.at[:, head(h, p * width)], dst_ref=dst.at[rows(p * BLOCK, BLOCK), head(h)],
            send_sem=fsend.at[which, h, p], recv_sem=frecv.at[which, h, p],
            device_id={"ctx": c, "mem": p}, device_id_type=MESH)

    def share(which, h, p, slot):
        src, dst = ((k_ref, kall), (v_ref, vall))[which]
        return pltpu.make_async_remote_copy(
            src_ref=src.at[:, head(h)], dst_ref=dst.at[slot, :, head(h)],
            send_sem=lsend.at[which, h, p], recv_sem=lrecv.at[which, h, slot],
            device_id={"ctx": p, "mem": m}, device_id_type=MESH)

    def forward(which, h, p, slot):
        buf = (kall, vall)[which]
        return pltpu.make_async_remote_copy(
            src_ref=buf.at[slot, :, head(h)], dst_ref=buf.at[slot, :, head(h)],
            send_sem=wsend.at[which, h], recv_sem=lrecv.at[which, h, slot],
            device_id={"ctx": p, "mem": m}, device_id_type=MESH)

    def apart(p):
        return c + p != 3 if four else p >= 0

    ways = ((1, 0, 0, 3), (2, 1, 0, 3), (3, 0, 1, 2), (3, 1, 1, 2)) if four else ()

    def pass_on(h):
        for at, which, slot, to in ways:
            @pl.when(c == at)
            def _(which=which, slot=slot, to=to):
                share(which, h, slot, slot).wait_recv()
                forward(which, h, to, slot).start()

    def part(h, p, slot):
        return pltpu.make_async_remote_copy(
            src_ref=parts.at[p, :, :, head(h)], dst_ref=recv.at[slot, :, :, head(h)],
            send_sem=psend.at[h, p], recv_sem=precv.at[h, slot],
            device_id={"ctx": p, "mem": m}, device_id_type=MESH)

    def owner_copy(h, r, src_c, src_i, base):
        return pltpu.make_async_remote_copy(
            src_ref=red.at[r, :, head(h)],
            dst_ref=out.at[src_c // nsub, rows(lax.rem(src_c, nsub) * rs, rs), head(h, base)],
            send_sem=osend.at[h, r], recv_sem=orecv.at[h, src_c, src_i],
            device_id={"ctx": group, "mem": r}, device_id_type=MESH)

    def start_head(h):
        def to_mem(d):
            p = lax.rem(m + d, n_mem)
            fetch(0, h, p).start()
            fetch(1, h, p).start()

        def to_ctx(p):
            @pl.when(apart(p))
            def _():
                share(0, h, p, c).start()
                share(1, h, p, c).start()

        loop(c + 1, n_ctx, to_ctx)
        loop(1, n_mem, to_mem)

    loop(0, heads, start_head)
    for copy in mine:
        copy.wait()

    causal = (lax.broadcasted_iota(jnp.int32, (tok, tok), 0)
              <= lax.broadcasted_iota(jnp.int32, (tok, tok), 1))

    def listed(b, r):
        hit = ids[b, 0] == r
        for j in range(1, n_list):
            hit = jnp.logical_or(hit, ids[b, j] == r)
        return jnp.where(hit, 0.0, NEG).astype(F32)

    def reduce_head(h):
        total = parts[c, :, :, head(h)].astype(F32)

        def add(d, total):
            src = lax.rem(c + d, n_ctx)
            part(h, src, src).wait_recv()
            return total + recv[src, :, :, head(h)].astype(F32)

        total = lax.fori_loop(1, n_ctx, add, total)
        red[:, :, head(h)] = total.astype(BF16)

        def send(d):
            r = lax.rem(m + d, n_mem)
            owner_copy(h, r, c, lax.rem(m, per), col0).start()

        loop(1, n_mem, send)

        @pl.when(group == c)
        def _():
            out[c // nsub, rows(lax.rem(c, nsub) * rs, rs), head(h, col0)] = red[m, :, head(h)]

        @pl.when(group != c)
        def _():
            owner_copy(h, m, c, lax.rem(m, per), col0).start()

    def share_of_gate(h):
        return 1.0 / (1.0 + jnp.exp(-jnp.full((1, HEAD_SIZE), gate[h], F32)))

    def row_max(s):
        return jnp.max(s, axis=0, keepdims=True)

    def row_sum(s):
        return jnp.sum(s, axis=0, keepdims=True)

    def gradient(h, share):
        return (share * do_ref[:, head(h)].astype(F32))

    def local_head(h):
        hc = head(h)
        q = q_ref[:, hc]
        keep = 1.0 - share_of_gate(h)
        dl = gradient(h, keep)
        dl_low = dl.astype(BF16)
        dl_t = dl.T

        def wait_local(j):
            for which in range(2):
                if four:
                    ahead = jnp.logical_or(jnp.logical_and(c == 1 + which, j == 0), jnp.logical_and(c == 3, j == 1))
                    pl.when(jnp.logical_not(ahead))(share(which, h, j, j).wait_recv)
                else:
                    share(which, h, j, j).wait_recv()

        loop(0, c, wait_local)

        s = jnp.where(causal, dot_nt(kall[c, :, hc], q) * scale2, NEG)
        s_loc[c] = s

        def scores(j, top):
            s = dot_nt(kall[j, :, hc], q) * scale2
            s_loc[j] = s
            return jnp.maximum(top, row_max(s))

        top = lax.fori_loop(0, c, scores, row_max(s))

        def gather(j, carry):
            total, acc = carry
            e = jnp.exp2(s_loc[j] - top)
            s_loc[j] = e
            return total + row_sum(e), acc + dot_tn(vall[j, :, hc], e.astype(BF16))

        total, acc = lax.fori_loop(0, c + 1, gather, (jnp.zeros((1, tok), F32), jnp.zeros((HEAD_SIZE, tok), F32)))
        inv = 1.0 / total
        local_out = acc * inv
        delta = row_sum(dl_t * local_out)

        def back(j, acc):
            dp = dot_nt(vall[j, :, hc], dl_low)
            ds = (s_loc[j] * inv) * (dp - delta)
            return acc + dot_tn(kall[j, :, hc], ds.astype(BF16))

        l_grad[rows(h * HEAD_SIZE, HEAD_SIZE), :] = lax.fori_loop(0, c + 1, back, jnp.zeros((HEAD_SIZE, tok), F32))
        l_out[rows(h * HEAD_SIZE, HEAD_SIZE), :] = keep[:, :1] * local_out

    def mem_head(h):
        hc = head(h)
        q = q_ref[:, hc]
        g = share_of_gate(h)
        dm = gradient(h, g)
        dm_low = dm.astype(BF16)
        dm_t = dm.T

        def wait_memory(d):
            p = lax.rem(m + d, n_mem)
            fetched(0, h, p).wait_recv()
            fetched(1, h, p).wait_recv()

        loop(1, n_mem, wait_memory)

        def mem_scores(i, top):
            s = dot_nt(fk[rows(i * chunk, chunk), hc], q) * scale2
            bias = [jnp.concatenate([jnp.full((1, BLOCK), listed(b, 2 * i + x), F32) for b in range(nqb)], axis=1)
                    for x in range(2)]
            s = jnp.concatenate([s[:BLOCK] + bias[0], s[BLOCK:] + bias[1]], axis=0)
            s_mem[i] = s
            return jnp.maximum(top, row_max(s))

        top = lax.fori_loop(0, n_chunk, mem_scores, jnp.full((1, tok), NEG, F32))

        def mem_gather(i, carry):
            total, acc = carry
            e = jnp.exp2(s_mem[i] - top)
            s_mem[i] = e
            return total + row_sum(e), acc + dot_tn(fv[rows(i * chunk, chunk), hc], e.astype(BF16))

        total, acc = lax.fori_loop(0, n_chunk, mem_gather,
                                   (jnp.zeros((1, tok), F32), jnp.zeros((HEAD_SIZE, tok), F32)))
        inv = 1.0 / total
        mem_out = acc * inv
        m_out[rows(h * HEAD_SIZE, HEAD_SIZE), :] = g[:, :1] * mem_out
        delta = row_sum(dm_t * mem_out)

        def mem_back(i, acc):
            dw = dot_nt(fv[rows(i * chunk, chunk), hc], dm_low)
            w = s_mem[i] * inv
            ds = (w * (dw - delta)).astype(BF16)
            part_k = (dot_nn(ds, q) * scale).astype(BF16)
            part_v = dot_nn(w.astype(BF16), dm_low).astype(BF16)
            for x in range(2):
                for s in range(nsub):
                    at = slice(x * BLOCK + s * rs, x * BLOCK + (s + 1) * rs)
                    parts[s, 2 * i + x, :, hc] = part_k[at]
                    parts[nsub + s, 2 * i + x, :, hc] = part_v[at]
            return acc + dot_tn(fk[rows(i * chunk, chunk), hc], ds)

        m_grad[rows(h * HEAD_SIZE, HEAD_SIZE), :] = lax.fori_loop(0, n_chunk, mem_back, jnp.zeros((HEAD_SIZE, tok), F32))
        loop(1, n_ctx, lambda d: part(h, lax.rem(c + d, n_ctx), c).start())

    def one_head(h):
        @pl.when(h < heads - 1)
        def _():
            pass_on(h + 1)

        mem_head(h)

        @pl.when(h > 0)
        def _():
            local_head(h - 1)
            reduce_head(h - 1)

    pass_on(0)
    loop(0, heads, one_head)
    local_head(heads - 1)
    reduce_head(heads - 1)
    mixed_ref[...] = (m_out[...] + l_out[...]).T.astype(BF16)
    qg_ref[...] = ((m_grad[...] + l_grad[...]) * scale).T.astype(BF16)

    def finish(h):
        def arrived(t):
            src_c, i = t // per, lax.rem(t, per)

            @pl.when(jnp.logical_or(src_c != c, c * per + i != m))
            def _():
                owner_copy(h, m, src_c, i, i * width).wait_recv()

        def sent_mem(d):
            p = lax.rem(m + d, n_mem)
            fetch(0, h, p).wait_send()
            fetch(1, h, p).wait_send()
            owner_copy(h, p, c, lax.rem(m, per), col0).wait_send()

        def sent_ctx(p):
            @pl.when(apart(p))
            def _():
                share(0, h, p, c).wait_send()
                share(1, h, p, c).wait_send()

        for at, which, slot, to in ways:
            pl.when(c == at)(forward(which, h, to, slot).wait_send)

        loop(0, n_ctx * per, arrived)
        loop(1, n_mem, sent_mem)
        loop(c + 1, n_ctx, sent_ctx)
        loop(1, n_ctx, lambda d: part(h, lax.rem(c + d, n_ctx), c).wait_send())

        @pl.when(group != c)
        def _():
            owner_copy(h, m, c, lax.rem(m, per), col0).wait_send()

    loop(0, heads, finish)
    gk_ref[...] = out[0]
    gv_ref[...] = out[1]


def hand_on(*refs):
    for src, dst in zip(refs[:4], refs[4:]):
        dst[...] = src[...]


def shards(n_ctx, n_mem, queries, keys, values, out_grad, mem_keys, mem_values, gate_logit, block_ids):
    tok, width = queries.shape
    columns = mem_keys.shape[1]
    heads = width // HEAD_SIZE
    rs = 2 * BLOCK // n_ctx
    mem_rows = n_mem * BLOCK
    vmem = pl.BlockSpec(memory_space=pltpu.VMEM)
    hbm = pl.BlockSpec(memory_space=pl.ANY)
    dma = pltpu.SemaphoreType.DMA
    pairs = (n_ctx + 1) * tok * tok * heads * HEAD_SIZE
    results = pl.pallas_call(
        functools.partial(kernel, n_ctx, n_mem),
        out_shape=(
            jax.ShapeDtypeStruct((tok, width), BF16),
            jax.ShapeDtypeStruct((tok, width), BF16),
            jax.ShapeDtypeStruct((BLOCK, columns // n_ctx), BF16),
            jax.ShapeDtypeStruct((BLOCK, columns // n_ctx), BF16),
        ),
        in_specs=[hbm] * 8,
        out_specs=(vmem, vmem, vmem, vmem),
        scratch_shapes=[
            pltpu.SMEM(block_ids.shape, jnp.int32),
            pltpu.SMEM(gate_logit.shape, F32),
            pltpu.VMEM((tok, width), BF16),
            pltpu.VMEM((tok, width), BF16),
            pltpu.VMEM((width, tok), F32),
            pltpu.VMEM((width, tok), F32),
            pltpu.VMEM((width, tok), F32),
            pltpu.VMEM((width, tok), F32),
            pltpu.VMEM((n_ctx, tok, width), BF16),
            pltpu.VMEM((n_ctx, tok, width), BF16),
            pltpu.VMEM((mem_rows, width), BF16),
            pltpu.VMEM((mem_rows, width), BF16),
            pltpu.VMEM((n_ctx, n_mem, rs, width), BF16),
            pltpu.VMEM((n_ctx, n_mem, rs, width), BF16),
            pltpu.VMEM((n_mem, rs, width), BF16),
            pltpu.VMEM((2, BLOCK, columns // n_ctx), BF16),
            pltpu.VMEM((n_ctx, tok, tok), F32),
            pltpu.VMEM((mem_rows // (2 * BLOCK), 2 * BLOCK, tok), F32),
            dma((8,)),
            dma((2, heads, n_mem)), dma((2, heads, n_mem)),
            dma((2, heads, n_ctx)), dma((2, heads, n_ctx)), dma((2, heads)),
            dma((heads, n_ctx)), dma((heads, n_ctx)),
            dma((heads, n_mem)), dma((heads, n_ctx, n_mem // n_ctx)),
        ],
        compiler_params=pltpu.CompilerParams(
            collective_id=0, has_side_effects=True, vmem_limit_bytes=62 * 1024 * 1024
        ),
        cost_estimate=pl.CostEstimate(
            flops=8 * pairs, bytes_accessed=8 * 1024 * 1024, transcendentals=4 * tok * tok * heads
        ),
    )(block_ids, gate_logit, queries, keys, values, out_grad, mem_keys, mem_values)
    return pl.pallas_call(
        hand_on,
        out_shape=tuple(jax.ShapeDtypeStruct(r.shape, r.dtype) for r in results),
        in_specs=[vmem] * 4,
        out_specs=(vmem,) * 4,
    )(*results)


def solution(mesh):
    in_specs = (
        P("ctx", "mem"),
        P("ctx", "mem"),
        P("ctx", "mem"),
        P("ctx", "mem"),
        P("mem", None),
        P("mem", None),
        P("mem"),
        P("ctx", None),
    )
    out_specs = (P("ctx", "mem"), P("ctx", "mem"), P("mem", "ctx"), P("mem", "ctx"))
    body = functools.partial(shards, mesh.shape["ctx"], mesh.shape["mem"])
    return jax.shard_map(body, mesh=mesh, in_specs=in_specs, out_specs=out_specs, check_vma=False)
```

```python
import functools
import math

import jax
import jax.numpy as jnp
from jax import lax
from jax.experimental import pallas as pl
from jax.experimental.pallas import tpu as pltpu
from jax.sharding import PartitionSpec as P

HEAD_SIZE = 128
BLOCK = 128
MESH = pl.DeviceIdType.MESH
NEG = -1e30
F32 = jnp.float32
BF16 = jnp.bfloat16


def dot_nt(a, b):
    return lax.dot_general(a, b, (((1,), (1,)), ((), ())), preferred_element_type=F32)


def dot_nn(a, b):
    return lax.dot_general(a, b, (((1,), (0,)), ((), ())), preferred_element_type=F32)


def dot_tn(a, b):
    return lax.dot_general(a, b, (((0,), (0,)), ((), ())), preferred_element_type=F32)


def loop(low, high, body):
    def step(i, carry):
        body(i)
        return carry

    lax.fori_loop(low, high, step, 0)


def kernel(n_ctx, n_mem, ids_in, gate_in, q_in, k_ref, v_ref, do_in, mk_ref, mv_ref,
           mixed_ref, qg_ref, gk_ref, gv_ref,
           ids, gate, q_ref, do_ref, l_out, l_grad, m_out, m_grad, kall, vall, fk, fv, parts, recv, red, out, s_loc, s_mem,
           own_sem, fsend, frecv, lsend, lrecv, wsend, psend, precv, osend, orecv):
    c = lax.axis_index("ctx")
    m = lax.axis_index("mem")
    tok, width = q_in.shape
    heads = width // HEAD_SIZE
    nqb = tok // BLOCK
    n_list = ids.shape[1]
    per = n_mem // n_ctx
    nsub = n_ctx // 2
    rs = BLOCK // nsub
    group = m // per
    col0 = lax.rem(m, per) * width
    scale = HEAD_SIZE ** -0.5
    scale2 = scale * math.log2(math.e)
    chunk = 2 * BLOCK
    n_chunk = n_mem * BLOCK // chunk
    four = n_ctx == 4

    def head(h, base=0):
        return pl.ds(pl.multiple_of(base + h * HEAD_SIZE, HEAD_SIZE), HEAD_SIZE)

    def rows(start, size):
        return pl.ds(pl.multiple_of(start, size), size)

    barrier = pltpu.get_barrier_semaphore()

    def greet(ctx, mem):
        pl.semaphore_signal(barrier, inc=1, device_id={"ctx": ctx, "mem": mem}, device_id_type=MESH)

    loop(1, n_mem, lambda d: greet(c, lax.rem(m + d, n_mem)))
    loop(1, n_ctx, lambda d: greet(lax.rem(c + d, n_ctx), m))

    def greet_owner(t):
        src_c, src_m = t // per, c * per + lax.rem(t, per)

        @pl.when(jnp.logical_or(src_c != c, src_m != m))
        def _():
            greet(src_c, src_m)

    loop(0, n_ctx * per, greet_owner)
    own_k = pltpu.make_async_copy(mk_ref.at[:, rows(m * width, width)], fk.at[rows(m * BLOCK, BLOCK)], own_sem.at[0])
    own_v = pltpu.make_async_copy(mv_ref.at[:, rows(m * width, width)], fv.at[rows(m * BLOCK, BLOCK)], own_sem.at[1])
    mine = [
        pltpu.make_async_copy(ids_in, ids, own_sem.at[2]),
        pltpu.make_async_copy(gate_in, gate, own_sem.at[3]),
        pltpu.make_async_copy(q_in, q_ref, own_sem.at[4]),
        pltpu.make_async_copy(do_in, do_ref, own_sem.at[5]),
        pltpu.make_async_copy(k_ref, kall.at[c], own_sem.at[6]),
        pltpu.make_async_copy(v_ref, vall.at[c], own_sem.at[7]),
        own_k,
        own_v,
    ]
    for copy in mine:
        copy.start()
    pl.semaphore_wait(barrier, n_mem - 1 + n_ctx - 1 + n_mem - jnp.where(group == c, 1, 0))

    def fetch(which, h, p):
        src, dst = ((mk_ref, fk), (mv_ref, fv))[which]
        return pltpu.make_async_remote_copy(
            src_ref=src.at[:, head(h, p * width)], dst_ref=dst.at[rows(m * BLOCK, BLOCK), head(h)],
            send_sem=fsend.at[which, h, p], recv_sem=frecv.at[which, h, m],
            device_id={"ctx": c, "mem": p}, device_id_type=MESH)

    def fetched(which, h, p):
        src, dst = ((mk_ref, fk), (mv_ref, fv))[which]
        return pltpu.make_async_remote_copy(
            src_ref=src.at[:, head(h, p * width)], dst_ref=dst.at[rows(p * BLOCK, BLOCK), head(h)],
            send_sem=fsend.at[which, h, p], recv_sem=frecv.at[which, h, p],
            device_id={"ctx": c, "mem": p}, device_id_type=MESH)

    def share(which, h, p, slot):
        src, dst = ((k_ref, kall), (v_ref, vall))[which]
        return pltpu.make_async_remote_copy(
            src_ref=src.at[:, head(h)], dst_ref=dst.at[slot, :, head(h)],
            send_sem=lsend.at[which, h, p], recv_sem=lrecv.at[which, h, slot],
            device_id={"ctx": p, "mem": m}, device_id_type=MESH)

    def forward(which, h, p, slot):
        buf = (kall, vall)[which]
        return pltpu.make_async_remote_copy(
            src_ref=buf.at[slot, :, head(h)], dst_ref=buf.at[slot, :, head(h)],
            send_sem=wsend.at[which, h], recv_sem=lrecv.at[which, h, slot],
            device_id={"ctx": p, "mem": m}, device_id_type=MESH)

    def apart(p):
        return c + p != 3 if four else p >= 0

    ways = ((1, 0, 0, 3), (2, 1, 0, 3), (3, 0, 1, 2), (3, 1, 1, 2)) if four else ()

    def pass_on(h):
        for at, which, slot, to in ways:
            @pl.when(c == at)
            def _(which=which, slot=slot, to=to):
                share(which, h, slot, slot).wait_recv()
                forward(which, h, to, slot).start()

    def part(h, p, slot):
        return pltpu.make_async_remote_copy(
            src_ref=parts.at[p, :, :, head(h)], dst_ref=recv.at[slot, :, :, head(h)],
            send_sem=psend.at[h, p], recv_sem=precv.at[h, slot],
            device_id={"ctx": p, "mem": m}, device_id_type=MESH)

    def owner_copy(h, r, src_c, src_i, base):
        return pltpu.make_async_remote_copy(
            src_ref=red.at[r, :, head(h)],
            dst_ref=out.at[src_c // nsub, rows(lax.rem(src_c, nsub) * rs, rs), head(h, base)],
            send_sem=osend.at[h, r], recv_sem=orecv.at[h, src_c, src_i],
            device_id={"ctx": group, "mem": r}, device_id_type=MESH)

    def start_head(h):
        def to_mem(d):
            p = lax.rem(m + d, n_mem)
            fetch(0, h, p).start()
            fetch(1, h, p).start()

        def to_ctx(p):
            @pl.when(apart(p))
            def _():
                share(0, h, p, c).start()
                share(1, h, p, c).start()

        loop(c + 1, n_ctx, to_ctx)
        loop(1, n_mem, to_mem)

    loop(0, heads, start_head)
    for copy in mine:
        copy.wait()

    causal = (lax.broadcasted_iota(jnp.int32, (tok, tok), 0)
              <= lax.broadcasted_iota(jnp.int32, (tok, tok), 1))

    def listed(b, r):
        hit = ids[b, 0] == r
        for j in range(1, n_list):
            hit = jnp.logical_or(hit, ids[b, j] == r)
        return jnp.where(hit, 0.0, NEG).astype(F32)

    def reduce_head(h):
        total = parts[c, :, :, head(h)].astype(F32)

        def add(d, total):
            src = lax.rem(c + d, n_ctx)
            part(h, src, src).wait_recv()
            return total + recv[src, :, :, head(h)].astype(F32)

        total = lax.fori_loop(1, n_ctx, add, total)
        red[:, :, head(h)] = total.astype(BF16)

        def send(d):
            r = lax.rem(m + d, n_mem)
            owner_copy(h, r, c, lax.rem(m, per), col0).start()

        loop(1, n_mem, send)

        @pl.when(group == c)
        def _():
            out[c // nsub, rows(lax.rem(c, nsub) * rs, rs), head(h, col0)] = red[m, :, head(h)]

        @pl.when(group != c)
        def _():
            owner_copy(h, m, c, lax.rem(m, per), col0).start()

    def share_of_gate(h):
        return 1.0 / (1.0 + jnp.exp(-jnp.full((1, HEAD_SIZE), gate[h], F32)))

    def row_max(s):
        return jnp.max(s, axis=0, keepdims=True)

    def row_sum(s):
        return jnp.sum(s, axis=0, keepdims=True)

    def gradient(h, share):
        return (share * do_ref[:, head(h)].astype(F32))

    def local_head(h):
        hc = head(h)
        q = q_ref[:, hc]
        keep = 1.0 - share_of_gate(h)
        dl = gradient(h, keep)
        dl_low = dl.astype(BF16)
        dl_t = dl.T

        def wait_local(j):
            for which in range(2):
                if four:
                    ahead = jnp.logical_or(jnp.logical_and(c == 1 + which, j == 0), jnp.logical_and(c == 3, j == 1))
                    pl.when(jnp.logical_not(ahead))(share(which, h, j, j).wait_recv)
                else:
                    share(which, h, j, j).wait_recv()

        loop(0, c, wait_local)

        s = jnp.where(causal, dot_nt(kall[c, :, hc], q) * scale2, NEG)
        s_loc[c] = s

        def scores(j, top):
            s = dot_nt(kall[j, :, hc], q) * scale2
            s_loc[j] = s
            return jnp.maximum(top, row_max(s))

        top = lax.fori_loop(0, c, scores, row_max(s))

        def gather(j, carry):
            total, acc = carry
            e = jnp.exp2(s_loc[j] - top)
            s_loc[j] = e
            return total + row_sum(e), acc + dot_tn(vall[j, :, hc], e.astype(BF16))

        total, acc = lax.fori_loop(0, c + 1, gather, (jnp.zeros((1, tok), F32), jnp.zeros((HEAD_SIZE, tok), F32)))
        inv = 1.0 / total
        local_out = acc * inv
        delta = row_sum(dl_t * local_out)

        def back(j, acc):
            dp = dot_nt(vall[j, :, hc], dl_low)
            ds = (s_loc[j] * inv) * (dp - delta)
            return acc + dot_tn(kall[j, :, hc], ds.astype(BF16))

        l_grad[rows(h * HEAD_SIZE, HEAD_SIZE), :] = lax.fori_loop(0, c + 1, back, jnp.zeros((HEAD_SIZE, tok), F32))
        l_out[rows(h * HEAD_SIZE, HEAD_SIZE), :] = keep[:, :1] * local_out

    def mem_head(h):
        hc = head(h)
        q = q_ref[:, hc]
        g = share_of_gate(h)
        dm = gradient(h, g)
        dm_low = dm.astype(BF16)
        dm_t = dm.T

        def wait_memory(d):
            p = lax.rem(m + d, n_mem)
            fetched(0, h, p).wait_recv()
            fetched(1, h, p).wait_recv()

        loop(1, n_mem, wait_memory)

        def mem_scores(i, top):
            s = dot_nt(fk[rows(i * chunk, chunk), hc], q) * scale2
            bias = [jnp.concatenate([jnp.full((1, BLOCK), listed(b, 2 * i + x), F32) for b in range(nqb)], axis=1)
                    for x in range(2)]
            s = jnp.concatenate([s[:BLOCK] + bias[0], s[BLOCK:] + bias[1]], axis=0)
            s_mem[i] = s
            return jnp.maximum(top, row_max(s))

        top = lax.fori_loop(0, n_chunk, mem_scores, jnp.full((1, tok), NEG, F32))

        def mem_gather(i, carry):
            total, acc = carry
            e = jnp.exp2(s_mem[i] - top)
            s_mem[i] = e
            return total + row_sum(e), acc + dot_tn(fv[rows(i * chunk, chunk), hc], e.astype(BF16))

        total, acc = lax.fori_loop(0, n_chunk, mem_gather,
                                   (jnp.zeros((1, tok), F32), jnp.zeros((HEAD_SIZE, tok), F32)))
        inv = 1.0 / total
        mem_out = acc * inv
        m_out[rows(h * HEAD_SIZE, HEAD_SIZE), :] = g[:, :1] * mem_out
        delta = row_sum(dm_t * mem_out)

        def mem_back(i, acc):
            dw = dot_nt(fv[rows(i * chunk, chunk), hc], dm_low)
            w = s_mem[i] * inv
            ds = (w * (dw - delta)).astype(BF16)
            part_k = (dot_nn(ds, q) * scale).astype(BF16)
            part_v = dot_nn(w.astype(BF16), dm_low).astype(BF16)
            for x in range(2):
                for s in range(nsub):
                    at = slice(x * BLOCK + s * rs, x * BLOCK + (s + 1) * rs)
                    parts[s, 2 * i + x, :, hc] = part_k[at]
                    parts[nsub + s, 2 * i + x, :, hc] = part_v[at]
            return acc + dot_tn(fk[rows(i * chunk, chunk), hc], ds)

        m_grad[rows(h * HEAD_SIZE, HEAD_SIZE), :] = lax.fori_loop(0, n_chunk, mem_back, jnp.zeros((HEAD_SIZE, tok), F32))
        loop(1, n_ctx, lambda d: part(h, lax.rem(c + d, n_ctx), c).start())

    def one_head(h):
        @pl.when(h < heads - 1)
        def _():
            pass_on(h + 1)

        mem_head(h)
        local_head(h)
        reduce_head(h)

    pass_on(0)
    loop(0, heads, one_head)
    mixed_ref[...] = (m_out[...] + l_out[...]).T.astype(BF16)
    qg_ref[...] = ((m_grad[...] + l_grad[...]) * scale).T.astype(BF16)

    def finish(h):
        def arrived(t):
            src_c, i = t // per, lax.rem(t, per)

            @pl.when(jnp.logical_or(src_c != c, c * per + i != m))
            def _():
                owner_copy(h, m, src_c, i, i * width).wait_recv()

        def sent_mem(d):
            p = lax.rem(m + d, n_mem)
            fetch(0, h, p).wait_send()
            fetch(1, h, p).wait_send()
            owner_copy(h, p, c, lax.rem(m, per), col0).wait_send()

        def sent_ctx(p):
            @pl.when(apart(p))
            def _():
                share(0, h, p, c).wait_send()
                share(1, h, p, c).wait_send()

        for at, which, slot, to in ways:
            pl.when(c == at)(forward(which, h, to, slot).wait_send)

        loop(0, n_ctx * per, arrived)
        loop(1, n_mem, sent_mem)
        loop(c + 1, n_ctx, sent_ctx)
        loop(1, n_ctx, lambda d: part(h, lax.rem(c + d, n_ctx), c).wait_send())

        @pl.when(group != c)
        def _():
            owner_copy(h, m, c, lax.rem(m, per), col0).wait_send()

    loop(0, heads, finish)
    gk_ref[...] = out[0]
    gv_ref[...] = out[1]


def hand_on(*refs):
    for src, dst in zip(refs[:4], refs[4:]):
        dst[...] = src[...]


def shards(n_ctx, n_mem, queries, keys, values, out_grad, mem_keys, mem_values, gate_logit, block_ids):
    tok, width = queries.shape
    columns = mem_keys.shape[1]
    heads = width // HEAD_SIZE
    rs = 2 * BLOCK // n_ctx
    mem_rows = n_mem * BLOCK
    vmem = pl.BlockSpec(memory_space=pltpu.VMEM)
    hbm = pl.BlockSpec(memory_space=pl.ANY)
    dma = pltpu.SemaphoreType.DMA
    pairs = (n_ctx + 1) * tok * tok * heads * HEAD_SIZE
    results = pl.pallas_call(
        functools.partial(kernel, n_ctx, n_mem),
        out_shape=(
            jax.ShapeDtypeStruct((tok, width), BF16),
            jax.ShapeDtypeStruct((tok, width), BF16),
            jax.ShapeDtypeStruct((BLOCK, columns // n_ctx), BF16),
            jax.ShapeDtypeStruct((BLOCK, columns // n_ctx), BF16),
        ),
        in_specs=[hbm] * 8,
        out_specs=(vmem, vmem, vmem, vmem),
        scratch_shapes=[
            pltpu.SMEM(block_ids.shape, jnp.int32),
            pltpu.SMEM(gate_logit.shape, F32),
            pltpu.VMEM((tok, width), BF16),
            pltpu.VMEM((tok, width), BF16),
            pltpu.VMEM((width, tok), F32),
            pltpu.VMEM((width, tok), F32),
            pltpu.VMEM((width, tok), F32),
            pltpu.VMEM((width, tok), F32),
            pltpu.VMEM((n_ctx, tok, width), BF16),
            pltpu.VMEM((n_ctx, tok, width), BF16),
            pltpu.VMEM((mem_rows, width), BF16),
            pltpu.VMEM((mem_rows, width), BF16),
            pltpu.VMEM((n_ctx, n_mem, rs, width), BF16),
            pltpu.VMEM((n_ctx, n_mem, rs, width), BF16),
            pltpu.VMEM((n_mem, rs, width), BF16),
            pltpu.VMEM((2, BLOCK, columns // n_ctx), BF16),
            pltpu.VMEM((n_ctx, tok, tok), F32),
            pltpu.VMEM((mem_rows // (2 * BLOCK), 2 * BLOCK, tok), F32),
            dma((8,)),
            dma((2, heads, n_mem)), dma((2, heads, n_mem)),
            dma((2, heads, n_ctx)), dma((2, heads, n_ctx)), dma((2, heads)),
            dma((heads, n_ctx)), dma((heads, n_ctx)),
            dma((heads, n_mem)), dma((heads, n_ctx, n_mem // n_ctx)),
        ],
        compiler_params=pltpu.CompilerParams(
            collective_id=0, has_side_effects=True, vmem_limit_bytes=62 * 1024 * 1024
        ),
        cost_estimate=pl.CostEstimate(
            flops=8 * pairs, bytes_accessed=8 * 1024 * 1024, transcendentals=4 * tok * tok * heads
        ),
    )(block_ids, gate_logit, queries, keys, values, out_grad, mem_keys, mem_values)
    return pl.pallas_call(
        hand_on,
        out_shape=tuple(jax.ShapeDtypeStruct(r.shape, r.dtype) for r in results),
        in_specs=[vmem] * 4,
        out_specs=(vmem,) * 4,
    )(*results)


def solution(mesh):
    in_specs = (
        P("ctx", "mem"),
        P("ctx", "mem"),
        P("ctx", "mem"),
        P("ctx", "mem"),
        P("mem", None),
        P("mem", None),
        P("mem"),
        P("ctx", None),
    )
    out_specs = (P("ctx", "mem"), P("ctx", "mem"), P("mem", "ctx"), P("mem", "ctx"))
    body = functools.partial(shards, mesh.shape["ctx"], mesh.shape["mem"])
    return jax.shard_map(body, mesh=mesh, in_specs=in_specs, out_specs=out_specs, check_vma=False)
```

```python
import functools
import math

import jax
import jax.numpy as jnp
from jax import lax
from jax.experimental import pallas as pl
from jax.experimental.pallas import tpu as pltpu
from jax.sharding import PartitionSpec as P

HEAD_SIZE = 128
BLOCK = 128
MESH = pl.DeviceIdType.MESH
NEG = -1e30
F32 = jnp.float32
BF16 = jnp.bfloat16


def dot_nt(a, b):
    return lax.dot_general(a, b, (((1,), (1,)), ((), ())), preferred_element_type=F32)


def dot_nn(a, b):
    return lax.dot_general(a, b, (((1,), (0,)), ((), ())), preferred_element_type=F32)


def dot_tn(a, b):
    return lax.dot_general(a, b, (((0,), (0,)), ((), ())), preferred_element_type=F32)


def loop(low, high, body):
    def step(i, carry):
        body(i)
        return carry

    lax.fori_loop(low, high, step, 0)


def kernel(n_ctx, n_mem, ids_in, gate_in, q_in, k_ref, v_ref, do_in, mk_ref, mv_ref,
           mixed_ref, qg_ref, gk_ref, gv_ref,
           ids, gate, q_ref, do_ref, l_out, l_grad, m_out, m_grad, kall, vall, fk, fv, parts, recv, red, out, s_loc, s_mem,
           own_sem, fsend, frecv, lsend, lrecv, wsend, psend, precv, osend, orecv):
    c = lax.axis_index("ctx")
    m = lax.axis_index("mem")
    tok, width = q_in.shape
    heads = width // HEAD_SIZE
    nqb = tok // BLOCK
    n_list = ids.shape[1]
    per = n_mem // n_ctx
    nsub = n_ctx // 2
    rs = BLOCK // nsub
    group = m // per
    col0 = lax.rem(m, per) * width
    scale = HEAD_SIZE ** -0.5
    scale2 = scale * math.log2(math.e)
    chunk = 2 * BLOCK
    n_chunk = n_mem * BLOCK // chunk
    four = n_ctx == 4

    def head(h, base=0):
        return pl.ds(pl.multiple_of(base + h * HEAD_SIZE, HEAD_SIZE), HEAD_SIZE)

    def rows(start, size):
        return pl.ds(pl.multiple_of(start, size), size)

    barrier = pltpu.get_barrier_semaphore()

    def greet(ctx, mem):
        pl.semaphore_signal(barrier, inc=1, device_id={"ctx": ctx, "mem": mem}, device_id_type=MESH)

    loop(1, n_mem, lambda d: greet(c, lax.rem(m + d, n_mem)))
    loop(1, n_ctx, lambda d: greet(lax.rem(c + d, n_ctx), m))

    def greet_owner(t):
        src_c, src_m = t // per, c * per + lax.rem(t, per)

        @pl.when(jnp.logical_or(src_c != c, src_m != m))
        def _():
            greet(src_c, src_m)

    loop(0, n_ctx * per, greet_owner)
    own_k = pltpu.make_async_copy(mk_ref.at[:, rows(m * width, width)], fk.at[rows(m * BLOCK, BLOCK)], own_sem.at[0])
    own_v = pltpu.make_async_copy(mv_ref.at[:, rows(m * width, width)], fv.at[rows(m * BLOCK, BLOCK)], own_sem.at[1])
    mine = [
        pltpu.make_async_copy(ids_in, ids, own_sem.at[2]),
        pltpu.make_async_copy(gate_in, gate, own_sem.at[3]),
        pltpu.make_async_copy(q_in, q_ref, own_sem.at[4]),
        pltpu.make_async_copy(do_in, do_ref, own_sem.at[5]),
        pltpu.make_async_copy(k_ref, kall.at[c], own_sem.at[6]),
        pltpu.make_async_copy(v_ref, vall.at[c], own_sem.at[7]),
        own_k,
        own_v,
    ]
    for copy in mine:
        copy.start()
    pl.semaphore_wait(barrier, n_mem - 1 + n_ctx - 1 + n_mem - jnp.where(group == c, 1, 0))

    def fetch(which, h, p):
        src, dst = ((mk_ref, fk), (mv_ref, fv))[which]
        return pltpu.make_async_remote_copy(
            src_ref=src.at[:, head(h, p * width)], dst_ref=dst.at[rows(m * BLOCK, BLOCK), head(h)],
            send_sem=fsend.at[which, h, p], recv_sem=frecv.at[which, h, m],
            device_id={"ctx": c, "mem": p}, device_id_type=MESH)

    def fetched(which, h, p):
        src, dst = ((mk_ref, fk), (mv_ref, fv))[which]
        return pltpu.make_async_remote_copy(
            src_ref=src.at[:, head(h, p * width)], dst_ref=dst.at[rows(p * BLOCK, BLOCK), head(h)],
            send_sem=fsend.at[which, h, p], recv_sem=frecv.at[which, h, p],
            device_id={"ctx": c, "mem": p}, device_id_type=MESH)

    def share(which, h, p, slot):
        src, dst = ((k_ref, kall), (v_ref, vall))[which]
        return pltpu.make_async_remote_copy(
            src_ref=src.at[:, head(h)], dst_ref=dst.at[slot, :, head(h)],
            send_sem=lsend.at[which, h, p], recv_sem=lrecv.at[which, h, slot],
            device_id={"ctx": p, "mem": m}, device_id_type=MESH)

    def forward(which, h, p, slot):
        buf = (kall, vall)[which]
        return pltpu.make_async_remote_copy(
            src_ref=buf.at[slot, :, head(h)], dst_ref=buf.at[slot, :, head(h)],
            send_sem=wsend.at[which, h], recv_sem=lrecv.at[which, h, slot],
            device_id={"ctx": p, "mem": m}, device_id_type=MESH)

    def apart(p):
        return c + p != 3 if four else p >= 0

    ways = ((1, 0, 0, 3), (2, 1, 0, 3), (3, 0, 1, 2), (3, 1, 1, 2)) if four else ()

    def pass_on(h):
        for at, which, slot, to in ways:
            @pl.when(c == at)
            def _(which=which, slot=slot, to=to):
                share(which, h, slot, slot).wait_recv()
                forward(which, h, to, slot).start()

    def part(h, p, slot):
        return pltpu.make_async_remote_copy(
            src_ref=parts.at[p, :, :, head(h)], dst_ref=recv.at[slot, :, :, head(h)],
            send_sem=psend.at[h, p], recv_sem=precv.at[h, slot],
            device_id={"ctx": p, "mem": m}, device_id_type=MESH)

    def owner_copy(h, r, src_c, src_i, base):
        return pltpu.make_async_remote_copy(
            src_ref=red.at[r, :, head(h)],
            dst_ref=out.at[src_c // nsub, rows(lax.rem(src_c, nsub) * rs, rs), head(h, base)],
            send_sem=osend.at[h, r], recv_sem=orecv.at[h, src_c, src_i],
            device_id={"ctx": group, "mem": r}, device_id_type=MESH)

    def start_head(h):
        def to_mem(d):
            p = lax.rem(m + d, n_mem)
            fetch(0, h, p).start()
            fetch(1, h, p).start()

        def to_ctx(p):
            @pl.when(apart(p))
            def _():
                share(0, h, p, c).start()
                share(1, h, p, c).start()

        loop(c + 1, n_ctx, to_ctx)
        loop(1, n_mem, to_mem)

    loop(0, heads, start_head)
    for copy in mine:
        copy.wait()

    causal = (lax.broadcasted_iota(jnp.int32, (tok, tok), 0)
              <= lax.broadcasted_iota(jnp.int32, (tok, tok), 1))

    def listed(b, r):
        hit = ids[b, 0] == r
        for j in range(1, n_list):
            hit = jnp.logical_or(hit, ids[b, j] == r)
        return jnp.where(hit, 0.0, NEG).astype(F32)

    def reduce_head(h):
        total = parts[c, :, :, head(h)].astype(F32)

        def add(d, total):
            src = lax.rem(c + d, n_ctx)
            part(h, src, src).wait_recv()
            return total + recv[src, :, :, head(h)].astype(F32)

        total = lax.fori_loop(1, n_ctx, add, total)
        red[:, :, head(h)] = total.astype(BF16)

        def send(d):
            r = lax.rem(m + d, n_mem)
            owner_copy(h, r, c, lax.rem(m, per), col0).start()

        loop(1, n_mem, send)

        @pl.when(group == c)
        def _():
            out[c // nsub, rows(lax.rem(c, nsub) * rs, rs), head(h, col0)] = red[m, :, head(h)]

        @pl.when(group != c)
        def _():
            owner_copy(h, m, c, lax.rem(m, per), col0).start()

    def share_of_gate(h):
        return 1.0 / (1.0 + jnp.exp(-jnp.full((1, HEAD_SIZE), gate[h], F32)))

    def row_max(s):
        return jnp.max(s, axis=0, keepdims=True)

    def row_sum(s):
        return jnp.sum(s, axis=0, keepdims=True)

    def gradient(h, share):
        return (share * do_ref[:, head(h)].astype(F32))

    def local_head(h):
        hc = head(h)
        q = q_ref[:, hc]
        keep = 1.0 - share_of_gate(h)
        dl = gradient(h, keep)
        dl_low = dl.astype(BF16)
        dl_t = dl.T

        def wait_local(j):
            for which in range(2):
                if four:
                    ahead = jnp.logical_or(jnp.logical_and(c == 1 + which, j == 0), jnp.logical_and(c == 3, j == 1))
                    pl.when(jnp.logical_not(ahead))(share(which, h, j, j).wait_recv)
                else:
                    share(which, h, j, j).wait_recv()

        loop(0, c, wait_local)

        s = jnp.where(causal, dot_nt(kall[c, :, hc], q) * scale2, NEG)
        s_loc[c] = s

        def scores(j, top):
            s = dot_nt(kall[j, :, hc], q) * scale2
            s_loc[j] = s
            return jnp.maximum(top, row_max(s))

        top = lax.fori_loop(0, c, scores, row_max(s))

        def gather(j, carry):
            total, acc = carry
            e = jnp.exp2(s_loc[j] - top)
            s_loc[j] = e
            return total + row_sum(e), acc + dot_tn(vall[j, :, hc], e.astype(BF16))

        total, acc = lax.fori_loop(0, c + 1, gather, (jnp.zeros((1, tok), F32), jnp.zeros((HEAD_SIZE, tok), F32)))
        inv = 1.0 / total
        local_out = acc * inv
        delta = row_sum(dl_t * local_out)

        def back(j, acc):
            dp = dot_nt(vall[j, :, hc], dl_low)
            ds = (s_loc[j] * inv) * (dp - delta)
            return acc + dot_tn(kall[j, :, hc], ds.astype(BF16))

        l_grad[rows(h * HEAD_SIZE, HEAD_SIZE), :] = lax.fori_loop(0, c + 1, back, jnp.zeros((HEAD_SIZE, tok), F32))
        l_out[rows(h * HEAD_SIZE, HEAD_SIZE), :] = keep[:, :1] * local_out

    def mem_head(h):
        hc = head(h)
        q = q_ref[:, hc]
        g = share_of_gate(h)
        dm = gradient(h, g)
        dm_low = dm.astype(BF16)
        dm_t = dm.T

        def wait_memory(d):
            p = lax.rem(m + d, n_mem)
            fetched(0, h, p).wait_recv()
            fetched(1, h, p).wait_recv()

        loop(1, n_mem, wait_memory)

        def mem_scores(i, top):
            s = dot_nt(fk[rows(i * chunk, chunk), hc], q) * scale2
            bias = [jnp.concatenate([jnp.full((1, BLOCK), listed(b, 2 * i + x), F32) for b in range(nqb)], axis=1)
                    for x in range(2)]
            s = jnp.concatenate([s[:BLOCK] + bias[0], s[BLOCK:] + bias[1]], axis=0)
            s_mem[i] = s
            return jnp.maximum(top, row_max(s))

        top = lax.fori_loop(0, n_chunk, mem_scores, jnp.full((1, tok), NEG, F32))

        def mem_gather(i, carry):
            total, acc = carry
            e = jnp.exp2(s_mem[i] - top)
            s_mem[i] = e
            return total + row_sum(e), acc + dot_tn(fv[rows(i * chunk, chunk), hc], e.astype(BF16))

        total, acc = lax.fori_loop(0, n_chunk, mem_gather,
                                   (jnp.zeros((1, tok), F32), jnp.zeros((HEAD_SIZE, tok), F32)))
        inv = 1.0 / total
        mem_out = acc * inv
        m_out[rows(h * HEAD_SIZE, HEAD_SIZE), :] = g[:, :1] * mem_out
        delta = row_sum(dm_t * mem_out)

        def mem_back(i, acc):
            dw = dot_nt(fv[rows(i * chunk, chunk), hc], dm_low)
            w = s_mem[i] * inv
            ds = (w * (dw - delta)).astype(BF16)
            part_k = (dot_nn(ds, q) * scale).astype(BF16)
            part_v = dot_nn(w.astype(BF16), dm_low).astype(BF16)
            for x in range(2):
                for s in range(nsub):
                    at = slice(x * BLOCK + s * rs, x * BLOCK + (s + 1) * rs)
                    parts[s, 2 * i + x, :, hc] = part_k[at]
                    parts[nsub + s, 2 * i + x, :, hc] = part_v[at]
            return acc + dot_tn(fk[rows(i * chunk, chunk), hc], ds)

        m_grad[rows(h * HEAD_SIZE, HEAD_SIZE), :] = lax.fori_loop(0, n_chunk, mem_back, jnp.zeros((HEAD_SIZE, tok), F32))
        loop(1, n_ctx, lambda d: part(h, lax.rem(c + d, n_ctx), c).start())

    def one_head(h):
        @pl.when(h < heads - 1)
        def _():
            pass_on(h + 1)

        mem_head(h)

        @pl.when(h > 0)
        def _():
            local_head(h - 1)

        @pl.when(h > 1)
        def _():
            reduce_head(h - 2)

    pass_on(0)
    loop(0, heads, one_head)
    if heads > 1:
        reduce_head(heads - 2)
    local_head(heads - 1)
    reduce_head(heads - 1)
    mixed_ref[...] = (m_out[...] + l_out[...]).T.astype(BF16)
    qg_ref[...] = ((m_grad[...] + l_grad[...]) * scale).T.astype(BF16)

    def finish(h):
        def arrived(t):
            src_c, i = t // per, lax.rem(t, per)

            @pl.when(jnp.logical_or(src_c != c, c * per + i != m))
            def _():
                owner_copy(h, m, src_c, i, i * width).wait_recv()

        def sent_mem(d):
            p = lax.rem(m + d, n_mem)
            fetch(0, h, p).wait_send()
            fetch(1, h, p).wait_send()
            owner_copy(h, p, c, lax.rem(m, per), col0).wait_send()

        def sent_ctx(p):
            @pl.when(apart(p))
            def _():
                share(0, h, p, c).wait_send()
                share(1, h, p, c).wait_send()

        for at, which, slot, to in ways:
            pl.when(c == at)(forward(which, h, to, slot).wait_send)

        loop(0, n_ctx * per, arrived)
        loop(1, n_mem, sent_mem)
        loop(c + 1, n_ctx, sent_ctx)
        loop(1, n_ctx, lambda d: part(h, lax.rem(c + d, n_ctx), c).wait_send())

        @pl.when(group != c)
        def _():
            owner_copy(h, m, c, lax.rem(m, per), col0).wait_send()

    loop(0, heads, finish)
    gk_ref[...] = out[0]
    gv_ref[...] = out[1]


def hand_on(*refs):
    for src, dst in zip(refs[:4], refs[4:]):
        dst[...] = src[...]


def shards(n_ctx, n_mem, queries, keys, values, out_grad, mem_keys, mem_values, gate_logit, block_ids):
    tok, width = queries.shape
    columns = mem_keys.shape[1]
    heads = width // HEAD_SIZE
    rs = 2 * BLOCK // n_ctx
    mem_rows = n_mem * BLOCK
    vmem = pl.BlockSpec(memory_space=pltpu.VMEM)
    hbm = pl.BlockSpec(memory_space=pl.ANY)
    dma = pltpu.SemaphoreType.DMA
    pairs = (n_ctx + 1) * tok * tok * heads * HEAD_SIZE
    results = pl.pallas_call(
        functools.partial(kernel, n_ctx, n_mem),
        out_shape=(
            jax.ShapeDtypeStruct((tok, width), BF16),
            jax.ShapeDtypeStruct((tok, width), BF16),
            jax.ShapeDtypeStruct((BLOCK, columns // n_ctx), BF16),
            jax.ShapeDtypeStruct((BLOCK, columns // n_ctx), BF16),
        ),
        in_specs=[hbm] * 8,
        out_specs=(vmem, vmem, vmem, vmem),
        scratch_shapes=[
            pltpu.SMEM(block_ids.shape, jnp.int32),
            pltpu.SMEM(gate_logit.shape, F32),
            pltpu.VMEM((tok, width), BF16),
            pltpu.VMEM((tok, width), BF16),
            pltpu.VMEM((width, tok), F32),
            pltpu.VMEM((width, tok), F32),
            pltpu.VMEM((width, tok), F32),
            pltpu.VMEM((width, tok), F32),
            pltpu.VMEM((n_ctx, tok, width), BF16),
            pltpu.VMEM((n_ctx, tok, width), BF16),
            pltpu.VMEM((mem_rows, width), BF16),
            pltpu.VMEM((mem_rows, width), BF16),
            pltpu.VMEM((n_ctx, n_mem, rs, width), BF16),
            pltpu.VMEM((n_ctx, n_mem, rs, width), BF16),
            pltpu.VMEM((n_mem, rs, width), BF16),
            pltpu.VMEM((2, BLOCK, columns // n_ctx), BF16),
            pltpu.VMEM((n_ctx, tok, tok), F32),
            pltpu.VMEM((mem_rows // (2 * BLOCK), 2 * BLOCK, tok), F32),
            dma((8,)),
            dma((2, heads, n_mem)), dma((2, heads, n_mem)),
            dma((2, heads, n_ctx)), dma((2, heads, n_ctx)), dma((2, heads)),
            dma((heads, n_ctx)), dma((heads, n_ctx)),
            dma((heads, n_mem)), dma((heads, n_ctx, n_mem // n_ctx)),
        ],
        compiler_params=pltpu.CompilerParams(
            collective_id=0, has_side_effects=True, vmem_limit_bytes=62 * 1024 * 1024
        ),
        cost_estimate=pl.CostEstimate(
            flops=8 * pairs, bytes_accessed=8 * 1024 * 1024, transcendentals=4 * tok * tok * heads
        ),
    )(block_ids, gate_logit, queries, keys, values, out_grad, mem_keys, mem_values)
    return pl.pallas_call(
        hand_on,
        out_shape=tuple(jax.ShapeDtypeStruct(r.shape, r.dtype) for r in results),
        in_specs=[vmem] * 4,
        out_specs=(vmem,) * 4,
    )(*results)


def solution(mesh):
    in_specs = (
        P("ctx", "mem"),
        P("ctx", "mem"),
        P("ctx", "mem"),
        P("ctx", "mem"),
        P("mem", None),
        P("mem", None),
        P("mem"),
        P("ctx", None),
    )
    out_specs = (P("ctx", "mem"), P("ctx", "mem"), P("mem", "ctx"), P("mem", "ctx"))
    body = functools.partial(shards, mesh.shape["ctx"], mesh.shape["mem"])
    return jax.shard_map(body, mesh=mesh, in_specs=in_specs, out_specs=out_specs, check_vma=False)
```

```python
import functools
import math

import jax
import jax.numpy as jnp
from jax import lax
from jax.experimental import pallas as pl
from jax.experimental.pallas import tpu as pltpu
from jax.sharding import PartitionSpec as P

HEAD_SIZE = 128
BLOCK = 128
MESH = pl.DeviceIdType.MESH
NEG = -1e30
F32 = jnp.float32
BF16 = jnp.bfloat16


def dot_nt(a, b):
    return lax.dot_general(a, b, (((1,), (1,)), ((), ())), preferred_element_type=F32)


def dot_nn(a, b):
    return lax.dot_general(a, b, (((1,), (0,)), ((), ())), preferred_element_type=F32)


def dot_tn(a, b):
    return lax.dot_general(a, b, (((0,), (0,)), ((), ())), preferred_element_type=F32)


def loop(low, high, body):
    def step(i, carry):
        body(i)
        return carry

    lax.fori_loop(low, high, step, 0)


def kernel(n_ctx, n_mem, ids_in, gate_in, q_in, k_ref, v_ref, do_in, mk_ref, mv_ref,
           mixed_ref, qg_ref, gk_ref, gv_ref,
           ids, gate, q_ref, do_ref, l_out, l_grad, m_out, m_grad, kall, vall, fk, fv, parts, recv, red, out, s_loc, s_mem,
           own_sem, fsend, frecv, lsend, lrecv, wsend, psend, precv, osend, orecv):
    c = lax.axis_index("ctx")
    m = lax.axis_index("mem")
    tok, width = q_in.shape
    heads = width // HEAD_SIZE
    nqb = tok // BLOCK
    n_list = ids.shape[1]
    per = n_mem // n_ctx
    nsub = n_ctx // 2
    rs = BLOCK // nsub
    group = m // per
    col0 = lax.rem(m, per) * width
    scale = HEAD_SIZE ** -0.5
    scale2 = scale * math.log2(math.e)
    chunk = 2 * BLOCK
    n_chunk = n_mem * BLOCK // chunk
    four = n_ctx == 4

    def head(h, base=0):
        return pl.ds(pl.multiple_of(base + h * HEAD_SIZE, HEAD_SIZE), HEAD_SIZE)

    def rows(start, size):
        return pl.ds(pl.multiple_of(start, size), size)

    barrier = pltpu.get_barrier_semaphore()

    def greet(ctx, mem):
        pl.semaphore_signal(barrier, inc=1, device_id={"ctx": ctx, "mem": mem}, device_id_type=MESH)

    loop(1, n_mem, lambda d: greet(c, lax.rem(m + d, n_mem)))
    loop(1, n_ctx, lambda d: greet(lax.rem(c + d, n_ctx), m))

    def greet_owner(t):
        src_c, src_m = t // per, c * per + lax.rem(t, per)

        @pl.when(jnp.logical_or(src_c != c, src_m != m))
        def _():
            greet(src_c, src_m)

    loop(0, n_ctx * per, greet_owner)
    own_k = pltpu.make_async_copy(mk_ref.at[:, rows(m * width, width)], fk.at[rows(m * BLOCK, BLOCK)], own_sem.at[0])
    own_v = pltpu.make_async_copy(mv_ref.at[:, rows(m * width, width)], fv.at[rows(m * BLOCK, BLOCK)], own_sem.at[1])
    mine = [
        pltpu.make_async_copy(ids_in, ids, own_sem.at[2]),
        pltpu.make_async_copy(gate_in, gate, own_sem.at[3]),
        pltpu.make_async_copy(q_in, q_ref, own_sem.at[4]),
        pltpu.make_async_copy(do_in, do_ref, own_sem.at[5]),
        pltpu.make_async_copy(k_ref, kall.at[c], own_sem.at[6]),
        pltpu.make_async_copy(v_ref, vall.at[c], own_sem.at[7]),
        own_k,
        own_v,
    ]
    for copy in mine:
        copy.start()
    pl.semaphore_wait(barrier, n_mem - 1 + n_ctx - 1 + n_mem - jnp.where(group == c, 1, 0))

    def fetch(which, h, p):
        src, dst = ((mk_ref, fk), (mv_ref, fv))[which]
        return pltpu.make_async_remote_copy(
            src_ref=src.at[:, head(h, p * width)], dst_ref=dst.at[rows(m * BLOCK, BLOCK), head(h)],
            send_sem=fsend.at[which, h, p], recv_sem=frecv.at[which, h, m],
            device_id={"ctx": c, "mem": p}, device_id_type=MESH)

    def fetched(which, h, p):
        src, dst = ((mk_ref, fk), (mv_ref, fv))[which]
        return pltpu.make_async_remote_copy(
            src_ref=src.at[:, head(h, p * width)], dst_ref=dst.at[rows(p * BLOCK, BLOCK), head(h)],
            send_sem=fsend.at[which, h, p], recv_sem=frecv.at[which, h, p],
            device_id={"ctx": c, "mem": p}, device_id_type=MESH)

    def share(which, h, p, slot):
        src, dst = ((k_ref, kall), (v_ref, vall))[which]
        return pltpu.make_async_remote_copy(
            src_ref=src.at[:, head(h)], dst_ref=dst.at[slot, :, head(h)],
            send_sem=lsend.at[which, h, p], recv_sem=lrecv.at[which, h, slot],
            device_id={"ctx": p, "mem": m}, device_id_type=MESH)

    def forward(which, h, p, slot):
        buf = (kall, vall)[which]
        return pltpu.make_async_remote_copy(
            src_ref=buf.at[slot, :, head(h)], dst_ref=buf.at[slot, :, head(h)],
            send_sem=wsend.at[which, h], recv_sem=lrecv.at[which, h, slot],
            device_id={"ctx": p, "mem": m}, device_id_type=MESH)

    def apart(p):
        return c + p != 3 if four else p >= 0

    ways = ((1, 0, 0, 3), (2, 1, 0, 3), (3, 0, 1, 2), (3, 1, 1, 2)) if four else ()

    def pass_on(h):
        for at, which, slot, to in ways:
            @pl.when(c == at)
            def _(which=which, slot=slot, to=to):
                share(which, h, slot, slot).wait_recv()
                forward(which, h, to, slot).start()

    def part(h, p, slot):
        return pltpu.make_async_remote_copy(
            src_ref=parts.at[p, :, :, head(h)], dst_ref=recv.at[slot, :, :, head(h)],
            send_sem=psend.at[h, p], recv_sem=precv.at[h, slot],
            device_id={"ctx": p, "mem": m}, device_id_type=MESH)

    def owner_copy(h, r, src_c, src_i, base):
        return pltpu.make_async_remote_copy(
            src_ref=red.at[r, :, head(h)],
            dst_ref=out.at[src_c // nsub, rows(lax.rem(src_c, nsub) * rs, rs), head(h, base)],
            send_sem=osend.at[h, r], recv_sem=orecv.at[h, src_c, src_i],
            device_id={"ctx": group, "mem": r}, device_id_type=MESH)

    def start_head(h):
        def to_mem(d):
            p = lax.rem(m + d, n_mem)
            fetch(0, h, p).start()
            fetch(1, h, p).start()

        def to_ctx(p):
            @pl.when(apart(p))
            def _():
                share(0, h, p, c).start()
                share(1, h, p, c).start()

        loop(1, n_mem, to_mem)
        loop(c + 1, n_ctx, to_ctx)

    loop(0, heads, start_head)
    for copy in mine:
        copy.wait()

    causal = (lax.broadcasted_iota(jnp.int32, (tok, tok), 0)
              <= lax.broadcasted_iota(jnp.int32, (tok, tok), 1))

    def listed(b, r):
        hit = ids[b, 0] == r
        for j in range(1, n_list):
            hit = jnp.logical_or(hit, ids[b, j] == r)
        return jnp.where(hit, 0.0, NEG).astype(F32)

    def reduce_head(h):
        total = parts[c, :, :, head(h)].astype(F32)

        def add(d, total):
            src = lax.rem(c + d, n_ctx)
            part(h, src, src).wait_recv()
            return total + recv[src, :, :, head(h)].astype(F32)

        total = lax.fori_loop(1, n_ctx, add, total)
        red[:, :, head(h)] = total.astype(BF16)

        def send(d):
            r = lax.rem(m + d, n_mem)
            owner_copy(h, r, c, lax.rem(m, per), col0).start()

        loop(1, n_mem, send)

        @pl.when(group == c)
        def _():
            out[c // nsub, rows(lax.rem(c, nsub) * rs, rs), head(h, col0)] = red[m, :, head(h)]

        @pl.when(group != c)
        def _():
            owner_copy(h, m, c, lax.rem(m, per), col0).start()

    def share_of_gate(h):
        return 1.0 / (1.0 + jnp.exp(-jnp.full((1, HEAD_SIZE), gate[h], F32)))

    def row_max(s):
        return jnp.max(s, axis=0, keepdims=True)

    def row_sum(s):
        return jnp.sum(s, axis=0, keepdims=True)

    def gradient(h, share):
        return (share * do_ref[:, head(h)].astype(F32))

    def local_head(h):
        hc = head(h)
        q = q_ref[:, hc]
        keep = 1.0 - share_of_gate(h)
        dl = gradient(h, keep)
        dl_low = dl.astype(BF16)
        dl_t = dl.T

        def wait_local(j):
            for which in range(2):
                if four:
                    ahead = jnp.logical_or(jnp.logical_and(c == 1 + which, j == 0), jnp.logical_and(c == 3, j == 1))
                    pl.when(jnp.logical_not(ahead))(share(which, h, j, j).wait_recv)
                else:
                    share(which, h, j, j).wait_recv()

        loop(0, c, wait_local)

        s = jnp.where(causal, dot_nt(kall[c, :, hc], q) * scale2, NEG)
        s_loc[c] = s

        def scores(j, top):
            s = dot_nt(kall[j, :, hc], q) * scale2
            s_loc[j] = s
            return jnp.maximum(top, row_max(s))

        top = lax.fori_loop(0, c, scores, row_max(s))

        def gather(j, carry):
            total, acc = carry
            e = jnp.exp2(s_loc[j] - top)
            s_loc[j] = e
            return total + row_sum(e), acc + dot_tn(vall[j, :, hc], e.astype(BF16))

        total, acc = lax.fori_loop(0, c + 1, gather, (jnp.zeros((1, tok), F32), jnp.zeros((HEAD_SIZE, tok), F32)))
        inv = 1.0 / total
        local_out = acc * inv
        delta = row_sum(dl_t * local_out)

        def back(j, acc):
            dp = dot_nt(vall[j, :, hc], dl_low)
            ds = (s_loc[j] * inv) * (dp - delta)
            return acc + dot_tn(kall[j, :, hc], ds.astype(BF16))

        l_grad[rows(h * HEAD_SIZE, HEAD_SIZE), :] = lax.fori_loop(0, c + 1, back, jnp.zeros((HEAD_SIZE, tok), F32))
        l_out[rows(h * HEAD_SIZE, HEAD_SIZE), :] = keep[:, :1] * local_out

    def mem_head(h):
        hc = head(h)
        q = q_ref[:, hc]
        g = share_of_gate(h)
        dm = gradient(h, g)
        dm_low = dm.astype(BF16)
        dm_t = dm.T

        def wait_memory(d):
            p = lax.rem(m + d, n_mem)
            fetched(0, h, p).wait_recv()
            fetched(1, h, p).wait_recv()

        loop(1, n_mem, wait_memory)

        def mem_scores(i, top):
            s = dot_nt(fk[rows(i * chunk, chunk), hc], q) * scale2
            bias = [jnp.concatenate([jnp.full((1, BLOCK), listed(b, 2 * i + x), F32) for b in range(nqb)], axis=1)
                    for x in range(2)]
            s = jnp.concatenate([s[:BLOCK] + bias[0], s[BLOCK:] + bias[1]], axis=0)
            s_mem[i] = s
            return jnp.maximum(top, row_max(s))

        top = lax.fori_loop(0, n_chunk, mem_scores, jnp.full((1, tok), NEG, F32))

        def mem_gather(i, carry):
            total, acc = carry
            e = jnp.exp2(s_mem[i] - top)
            s_mem[i] = e
            return total + row_sum(e), acc + dot_tn(fv[rows(i * chunk, chunk), hc], e.astype(BF16))

        total, acc = lax.fori_loop(0, n_chunk, mem_gather,
                                   (jnp.zeros((1, tok), F32), jnp.zeros((HEAD_SIZE, tok), F32)))
        inv = 1.0 / total
        mem_out = acc * inv
        m_out[rows(h * HEAD_SIZE, HEAD_SIZE), :] = g[:, :1] * mem_out
        delta = row_sum(dm_t * mem_out)

        def mem_back(i, acc):
            dw = dot_nt(fv[rows(i * chunk, chunk), hc], dm_low)
            w = s_mem[i] * inv
            ds = (w * (dw - delta)).astype(BF16)
            part_k = (dot_nn(ds, q) * scale).astype(BF16)
            part_v = dot_nn(w.astype(BF16), dm_low).astype(BF16)
            for x in range(2):
                for s in range(nsub):
                    at = slice(x * BLOCK + s * rs, x * BLOCK + (s + 1) * rs)
                    parts[s, 2 * i + x, :, hc] = part_k[at]
                    parts[nsub + s, 2 * i + x, :, hc] = part_v[at]
            return acc + dot_tn(fk[rows(i * chunk, chunk), hc], ds)

        m_grad[rows(h * HEAD_SIZE, HEAD_SIZE), :] = lax.fori_loop(0, n_chunk, mem_back, jnp.zeros((HEAD_SIZE, tok), F32))
        loop(1, n_ctx, lambda d: part(h, lax.rem(c + d, n_ctx), c).start())

    def one_head(h):
        @pl.when(h < heads - 1)
        def _():
            pass_on(h + 1)

        mem_head(h)

        @pl.when(h > 0)
        def _():
            local_head(h - 1)
            reduce_head(h - 1)

    pass_on(0)
    loop(0, heads, one_head)
    local_head(heads - 1)
    reduce_head(heads - 1)
    mixed_ref[...] = (m_out[...] + l_out[...]).T.astype(BF16)
    qg_ref[...] = ((m_grad[...] + l_grad[...]) * scale).T.astype(BF16)

    def finish(h):
        def arrived(t):
            src_c, i = t // per, lax.rem(t, per)

            @pl.when(jnp.logical_or(src_c != c, c * per + i != m))
            def _():
                owner_copy(h, m, src_c, i, i * width).wait_recv()

        def sent_mem(d):
            p = lax.rem(m + d, n_mem)
            fetch(0, h, p).wait_send()
            fetch(1, h, p).wait_send()
            owner_copy(h, p, c, lax.rem(m, per), col0).wait_send()

        def sent_ctx(p):
            @pl.when(apart(p))
            def _():
                share(0, h, p, c).wait_send()
                share(1, h, p, c).wait_send()

        for at, which, slot, to in ways:
            pl.when(c == at)(forward(which, h, to, slot).wait_send)

        loop(0, n_ctx * per, arrived)
        loop(1, n_mem, sent_mem)
        loop(c + 1, n_ctx, sent_ctx)
        loop(1, n_ctx, lambda d: part(h, lax.rem(c + d, n_ctx), c).wait_send())

        @pl.when(group != c)
        def _():
            owner_copy(h, m, c, lax.rem(m, per), col0).wait_send()

    loop(0, heads, finish)
    gk_ref[...] = out[0]
    gv_ref[...] = out[1]


def hand_on(*refs):
    for src, dst in zip(refs[:4], refs[4:]):
        dst[...] = src[...]


def shards(n_ctx, n_mem, queries, keys, values, out_grad, mem_keys, mem_values, gate_logit, block_ids):
    tok, width = queries.shape
    columns = mem_keys.shape[1]
    heads = width // HEAD_SIZE
    rs = 2 * BLOCK // n_ctx
    mem_rows = n_mem * BLOCK
    vmem = pl.BlockSpec(memory_space=pltpu.VMEM)
    hbm = pl.BlockSpec(memory_space=pl.ANY)
    dma = pltpu.SemaphoreType.DMA
    pairs = (n_ctx + 1) * tok * tok * heads * HEAD_SIZE
    results = pl.pallas_call(
        functools.partial(kernel, n_ctx, n_mem),
        out_shape=(
            jax.ShapeDtypeStruct((tok, width), BF16),
            jax.ShapeDtypeStruct((tok, width), BF16),
            jax.ShapeDtypeStruct((BLOCK, columns // n_ctx), BF16),
            jax.ShapeDtypeStruct((BLOCK, columns // n_ctx), BF16),
        ),
        in_specs=[hbm] * 8,
        out_specs=(vmem, vmem, vmem, vmem),
        scratch_shapes=[
            pltpu.SMEM(block_ids.shape, jnp.int32),
            pltpu.SMEM(gate_logit.shape, F32),
            pltpu.VMEM((tok, width), BF16),
            pltpu.VMEM((tok, width), BF16),
            pltpu.VMEM((width, tok), F32),
            pltpu.VMEM((width, tok), F32),
            pltpu.VMEM((width, tok), F32),
            pltpu.VMEM((width, tok), F32),
            pltpu.VMEM((n_ctx, tok, width), BF16),
            pltpu.VMEM((n_ctx, tok, width), BF16),
            pltpu.VMEM((mem_rows, width), BF16),
            pltpu.VMEM((mem_rows, width), BF16),
            pltpu.VMEM((n_ctx, n_mem, rs, width), BF16),
            pltpu.VMEM((n_ctx, n_mem, rs, width), BF16),
            pltpu.VMEM((n_mem, rs, width), BF16),
            pltpu.VMEM((2, BLOCK, columns // n_ctx), BF16),
            pltpu.VMEM((n_ctx, tok, tok), F32),
            pltpu.VMEM((mem_rows // (2 * BLOCK), 2 * BLOCK, tok), F32),
            dma((8,)),
            dma((2, heads, n_mem)), dma((2, heads, n_mem)),
            dma((2, heads, n_ctx)), dma((2, heads, n_ctx)), dma((2, heads)),
            dma((heads, n_ctx)), dma((heads, n_ctx)),
            dma((heads, n_mem)), dma((heads, n_ctx, n_mem // n_ctx)),
        ],
        compiler_params=pltpu.CompilerParams(
            collective_id=0, has_side_effects=True, vmem_limit_bytes=62 * 1024 * 1024
        ),
        cost_estimate=pl.CostEstimate(
            flops=8 * pairs, bytes_accessed=8 * 1024 * 1024, transcendentals=4 * tok * tok * heads
        ),
    )(block_ids, gate_logit, queries, keys, values, out_grad, mem_keys, mem_values)
    return pl.pallas_call(
        hand_on,
        out_shape=tuple(jax.ShapeDtypeStruct(r.shape, r.dtype) for r in results),
        in_specs=[vmem] * 4,
        out_specs=(vmem,) * 4,
    )(*results)


def solution(mesh):
    in_specs = (
        P("ctx", "mem"),
        P("ctx", "mem"),
        P("ctx", "mem"),
        P("ctx", "mem"),
        P("mem", None),
        P("mem", None),
        P("mem"),
        P("ctx", None),
    )
    out_specs = (P("ctx", "mem"), P("ctx", "mem"), P("mem", "ctx"), P("mem", "ctx"))
    body = functools.partial(shards, mesh.shape["ctx"], mesh.shape["mem"])
    return jax.shard_map(body, mesh=mesh, in_specs=in_specs, out_specs=out_specs, check_vma=False)
```
